32 devices in a mesh: tile: 2 (over x), beam: 16 (over z, y, core).
Axes of the slice: x: 2, y: 2, z: 4, core: 2. Of those that a mesh axis runs over, the one named last changes fastest.
Arguments:
- echoes: bfloat16 [2, 2048, 8192], P(None, 'tile', 'beam'), may hold values from -160 to 160
- steer: bfloat16 [2, 2048, 2048], P(None, None, 'tile'), may hold values from -0.09375 to 0.09375
- code: bfloat16 [2, 8], replicated, may hold values from -1 to 1
- beam_order: int32 [2048], replicated, may hold values from 0 to 2047, each once
- dwell: int32 [2048], replicated, may hold values from 64 to 256, as said below
- code_len: int32 [2048], replicated, may hold values from 1 to 8, as said below
Outputs:
- spectrum: float32 [2048, 2, 32, 256], P(('tile', 'beam'))
The draws below stay inside these ranges and needn't reach their ends.
Inputs may be any that keep to these rules, and one draw needn't show every extreme that they name: dwell[b] counts the leading pulses that beam b keeps; some beam keeps all 256. `code_len`: some beam uses all 8 taps.
All inputs are finite; a program needn't handle non-finite values.
Results may differ from the reference program's by a relative error of at most 0.015.
Values may be sent and summed in bfloat16 or wider, within the bound.
No kernel may reach another device: no remote copies, remote signals or barrier semaphores. Data moves between devices by JAX's collectives and lax.ppermute only.
A program may use at most 64 MiB of HBM per device.

```python
import math
import jax
import jax.numpy as jnp
from jax import lax

C = 2048
B = 2048
G = 32
CODE = 8
P_SIZE = 256
N_TILE = 2


def draw_echoes(key, part):
    key_data, key_chan = jax.random.split(jax.random.fold_in(key, 3))
    chan = jnp.exp(jax.random.uniform(key_chan, (C,), jnp.float32) * math.log(10.0))
    ramp = jnp.arange(P_SIZE, dtype=jnp.float32) / max(P_SIZE - 1, 1)
    amp = jnp.exp(ramp * math.log(3.0))
    base = jnp.clip(jax.random.normal(key_data, (2, C, P_SIZE, G), jnp.float32), -4.0, 4.0)
    values = base * chan[None, :, None, None] * amp[None, None, :, None]
    return values.reshape(2, C, P_SIZE * G).astype(jnp.bfloat16)


def draw_dwell(key, part):
    key_vals, key_at = jax.random.split(jax.random.fold_in(key, 11))
    vals = jax.random.randint(key_vals, (B,), P_SIZE // 4, P_SIZE + 1)
    where = jax.random.randint(key_at, (), 0, B)
    return vals.at[where].set(P_SIZE)


def draw_code_len(key, part):
    key_vals, key_at = jax.random.split(jax.random.fold_in(key, 17))
    vals = jax.random.randint(key_vals, (B,), 1, CODE + 1)
    where = jax.random.randint(key_at, (), 0, B)
    return vals.at[where].set(CODE)


def levels(rng, shape, cuts, low, top_value):
    def one(axis_at, parts):
        heights = jax.random.uniform(jax.random.fold_in(jax.random.fold_in(rng, 6), axis_at), (parts,), jnp.float32, low / len(cuts), top_value / len(cuts))
        return jnp.repeat(jnp.exp(heights), shape[axis_at] // parts).reshape((-1,) + (1,) * (len(shape) - axis_at - 1))

    factor_of = one(*cuts[0])
    for cut in cuts[1:]:
        factor_of = factor_of * one(*cut)
    return factor_of


def normal_values(stream_key, dims, deviation, limit, shards=(), kind=jnp.bfloat16):
    factor_of = levels(stream_key, dims, shards, -0.22, 0.18) if shards else 1.0
    drawn = jax.random.normal(stream_key, dims, jnp.float32) * deviation * factor_of
    return jnp.minimum(jnp.maximum(drawn, -limit), limit).astype(kind)


def setup_inputs(seed: int = 0) -> dict:
    streams_of = jax.random.split(jax.random.key(seed), 7)
    echoes = draw_echoes(jax.random.fold_in(streams_of[6], 71), 0)
    steer = normal_values(streams_of[1], (2, B, C), (2 * C) ** -0.5, 0.09375, ((2, 2),))
    code = normal_values(streams_of[2], (2, CODE), 0.25, 1.0)
    beam_order = jax.random.permutation(streams_of[3], B).astype(jnp.int32)
    dwell = draw_dwell(jax.random.fold_in(streams_of[6], 71), 0)
    code_len = draw_code_len(jax.random.fold_in(streams_of[6], 71), 0)
    return dict(echoes=echoes, steer=steer, code=code, beam_order=beam_order, dwell=dwell, code_len=code_len)


def complex_block(weight_re, weight_im):
    upper = jnp.concatenate([weight_re, -weight_im], axis=1)
    lower = jnp.concatenate([weight_im, weight_re], axis=1)
    return jnp.stack([upper, lower], axis=1).reshape(2 * weight_re.shape[0], 2 * weight_re.shape[1])

def dft_rows(first, count, total):
    row_index = first + jnp.arange(count, dtype=jnp.int32)
    freqs = jnp.arange(total, dtype=jnp.int32)
    phase = row_index[:, None] * freqs[None, :] % total
    angle = phase.astype(jnp.float32) * (2.0 * math.pi / total)
    return (jnp.cos(angle), -jnp.sin(angle))

def compress(values, code, lens, limits, first_pulse):
    gates = values.shape[3]
    taps = code.shape[1]
    padded = jnp.pad(values, ((0, 0), (0, 0), (0, 0), (0, taps)))
    code_re = code[0].astype(jnp.float32)
    code_im = code[1].astype(jnp.float32)
    out_re = jnp.zeros((values.shape[0], values.shape[2], gates), jnp.float32)
    out_im = jnp.zeros((values.shape[0], values.shape[2], gates), jnp.float32)
    for tap in range(taps):
        live = (tap < lens).astype(jnp.float32)[:, None, None]
        shift_re = padded[:, 0, :, tap:tap + gates]
        shift_im = padded[:, 1, :, tap:tap + gates]
        out_re = out_re + live * (code_re[tap] * shift_re + code_im[tap] * shift_im)
        out_im = out_im + live * (code_re[tap] * shift_im - code_im[tap] * shift_re)
    pulse_index = first_pulse + jnp.arange(values.shape[2], dtype=jnp.int32)
    keep = (pulse_index[None, :] < limits[:, None]).astype(jnp.float32)[:, None, :, None]
    return (jnp.stack([out_re, out_im], axis=1) * keep).astype(jnp.bfloat16)

def reference(echoes, steer, code, beam_order, dwell, code_len):
    beam_total = steer.shape[1]
    chans = C // N_TILE
    columns = P_SIZE * G
    values = echoes.astype(jnp.float32)
    power = lax.optimization_barrier(jnp.sum(values * values, axis=(0, 2))) / (P_SIZE * G)
    gain = lax.rsqrt(power + 1e-05)
    ordered = jnp.take(steer, beam_order, axis=1)
    weights = (ordered.astype(jnp.float32) * gain).astype(jnp.bfloat16)
    blocks = [complex_block(weights[0, :, t * chans:(t + 1) * chans], weights[1, :, t * chans:(t + 1) * chans]) for t in range(N_TILE)]
    width = min(512, columns)
    count = columns // width

    def beam_cols(index):
        part = lax.dynamic_slice_in_dim(echoes, index * width, width, 2)
        total = jnp.zeros((beam_total, 2, width), jnp.float32)
        for t in range(N_TILE):
            flat = part[:, t * chans:(t + 1) * chans, :].reshape(2 * chans, width)
            term = jnp.dot(blocks[t], flat, preferred_element_type=jnp.float32).reshape(beam_total, 2, width)
            total = total + lax.optimization_barrier(term.astype(jnp.bfloat16)).astype(jnp.float32)
        return total.astype(jnp.bfloat16)
    pieces = lax.map(beam_cols, jnp.arange(count, dtype=jnp.int32))
    beams = jnp.transpose(pieces, (1, 2, 0, 3)).reshape(beam_total, 2, P_SIZE, G)
    lens = jnp.take(code_len, beam_order)
    limits = jnp.take(dwell, beam_order)
    table_re, table_im = dft_rows(0, P_SIZE, P_SIZE)
    group = min(64, beam_total)
    groups = beam_total // group

    def per_group(inputs):
        beam_part, lens_part, limits_part = inputs
        squeezed = compress(beam_part.astype(jnp.float32), code, lens_part, limits_part, 0).astype(jnp.float32)
        first = jnp.einsum('bcpg,pk->bcgk', squeezed, table_re, precision=lax.Precision.HIGHEST)
        second = jnp.einsum('bcpg,pk->bcgk', squeezed, table_im, precision=lax.Precision.HIGHEST)
        joined = jnp.stack([first[:, 0] - second[:, 1], first[:, 1] + second[:, 0]], axis=1)
        return joined * (1.0 / math.sqrt(P_SIZE))
    result = lax.map(per_group, (beams.reshape(groups, group, 2, P_SIZE, G), lens.reshape(groups, group), limits.reshape(groups, group)))
    return result.reshape(beam_total, 2, G, P_SIZE)
```

```python
import functools
import math

import jax
import jax.numpy as jnp
import numpy as np
from jax import lax
from jax.experimental import pallas as pl
from jax.experimental.pallas import tpu as pltpu
from jax.sharding import PartitionSpec as P

G = 32
EPS = 1e-05
SPLIT = (8, 8, 16)
NT = (((1,), (1,)), ((), ()))
TN = (((0,), (0,)), ((), ()))
VMEM = pl.BlockSpec(memory_space=pltpu.VMEM)
LIMIT = 40 * 1024 * 1024


def params():
    return pltpu.CompilerParams(vmem_limit_bytes=LIMIT)


def block_of(size, most):
    return max(n for n in range(1, min(size, most) + 1) if size % n == 0)


def chunks_of(gates):
    sizes = SPLIT if sum(SPLIT) == gates else (gates,)
    found, end = [], gates
    for size in sizes:
        found.append((end - size, size))
        end -= size
    return found


def prep_kernel(gates, echoes_ref, turned_ref, power_ref, order_ref):
    columns = order_ref.shape[0]
    pulses = columns // gates

    @pl.when(pl.program_id(0) == 0)
    def _():
        row = lax.broadcasted_iota(jnp.int32, (columns, columns), 0)
        col = lax.broadcasted_iota(jnp.int32, (columns, columns), 1)
        source = (row % pulses) * gates + row // pulses
        order_ref[...] = jnp.where(source == col, 1.0, 0.0).astype(jnp.bfloat16)

    power = None
    for part in range(2):
        turned = lax.dot_general(order_ref[...], echoes_ref[part], NT, preferred_element_type=jnp.float32)
        turned_ref[part] = turned.astype(jnp.bfloat16)
        term = jnp.sum(turned * turned, axis=0, keepdims=True)
        power = term if power is None else power + term
    power_ref[...] = power


def prep(echoes, gates):
    _, chans, columns = echoes.shape
    width = block_of(chans, 256)
    return pl.pallas_call(
        functools.partial(prep_kernel, gates),
        grid=(chans // width,),
        in_specs=[pl.BlockSpec((2, width, columns), lambda i: (0, i, 0))],
        out_specs=[
            pl.BlockSpec((2, columns, width), lambda i: (0, 0, i)),
            pl.BlockSpec((1, width), lambda i: (0, i)),
        ],
        out_shape=[
            jax.ShapeDtypeStruct((2, columns, chans), jnp.bfloat16),
            jax.ShapeDtypeStruct((1, chans), jnp.float32),
        ],
        scratch_shapes=[pltpu.VMEM((columns, columns), jnp.bfloat16)],
        compiler_params=params(),
        name="prep",
    )(echoes)


def beam_kernel(first, rows, samples, b_steps, turned_ref, power_ref, order_ref, steer_ref, *rest):
    out_refs, (scaled_ref, beams_ref) = rest[:-2], rest[-2:]
    step = pl.program_id(0)
    chans = power_ref.shape[1]
    wide = steer_ref.shape[1]

    @pl.when(step == 0)
    def _():
        gain = lax.rsqrt(power_ref[...] / samples + EPS)
        real = turned_ref[0, first : first + rows].astype(jnp.float32) * gain
        imag = turned_ref[1, first : first + rows].astype(jnp.float32) * gain
        scaled_ref[:rows, :chans] = real.astype(jnp.bfloat16)
        scaled_ref[:rows, chans:] = (-imag).astype(jnp.bfloat16)
        scaled_ref[rows:, :chans] = imag.astype(jnp.bfloat16)
        scaled_ref[rows:, chans:] = real.astype(jnp.bfloat16)

    @pl.when(step < b_steps)
    def _():
        total = lax.dot_general(scaled_ref[:, :chans], steer_ref[0], NT, preferred_element_type=jnp.float32)
        total += lax.dot_general(scaled_ref[:, chans:], steer_ref[1], NT, preferred_element_type=jnp.float32)
        beams_ref[:, pl.ds(pl.multiple_of(step * wide, wide), wide)] = total.astype(jnp.bfloat16)

    @pl.when(step >= b_steps)
    def _():
        beam_total, slots = beams_ref.shape[1], order_ref.shape[1]
        row = lax.broadcasted_iota(jnp.int32, (beam_total, slots), 0)
        pick = jnp.where(row == order_ref[...], 1.0, 0.0).astype(jnp.bfloat16)
        picked = jnp.dot(beams_ref[...], pick, preferred_element_type=jnp.float32).astype(jnp.bfloat16)
        per = (pl.num_programs(0) - b_steps) // len(out_refs)
        for index, out_ref in enumerate(out_refs):

            @pl.when((step - b_steps) // per == index)
            def _(out_ref=out_ref):
                out_ref[...] = picked


def form_beams(turned, power, order, steer, first, rows, samples, tiles):
    _, columns, chans = turned.shape
    beam_total = steer.shape[1]
    tile_beams = beam_total // tiles
    wide = block_of(beam_total, 512)
    slots = block_of(tile_beams, 512)
    b_steps, per = beam_total // wide, tile_beams // slots
    steps = b_steps + per * tiles

    def out_map(index):
        return lambda i: (0, jnp.clip(i - b_steps - index * per, 0, per - 1))

    return pl.pallas_call(
        functools.partial(beam_kernel, first, rows, samples, b_steps),
        grid=(steps,),
        in_specs=[
            pl.BlockSpec((2, columns, chans), lambda i: (0, 0, 0)),
            pl.BlockSpec((1, chans), lambda i: (0, 0)),
            pl.BlockSpec((1, slots), lambda i: (0, jnp.maximum(i - b_steps, 0))),
            pl.BlockSpec((2, wide, chans), lambda i: (0, jnp.minimum(i, b_steps - 1), 0)),
        ],
        out_specs=[pl.BlockSpec((2 * rows, slots), out_map(index)) for index in range(tiles)],
        out_shape=[jax.ShapeDtypeStruct((2 * rows, tile_beams), jnp.bfloat16)] * tiles,
        scratch_shapes=[
            pltpu.VMEM((2 * rows, 2 * chans), jnp.bfloat16),
            pltpu.VMEM((2 * rows, beam_total), jnp.bfloat16),
        ],
        compiler_params=params(),
        cost_estimate=pl.CostEstimate(
            flops=4 * rows * beam_total * (2 * chans + beam_total),
            bytes_accessed=steer.size * 2 + turned.size * 2 + 4 * rows * beam_total,
            transcendentals=0,
        ),
        name="beams",
    )(turned, power, order, steer)


def compress_kernel(pulses, taps, parts_in, halo, keep_ahead, own, code_ref, at_ref, lens_ref, limits_ref, *rest):
    part_refs, rest = rest[:parts_in], rest[parts_in:]
    if halo:
        ahead_ref, rest = rest[0], rest[1:]
    out_ref, rest = rest[0], rest[1:]
    if keep_ahead:
        beams_ref, rest = rest[0], rest[1:]
    (wide_ref,) = rest
    rows = part_refs[0].shape[0] // 2
    edge = (taps - 1) * pulses
    lanes = part_refs[0].shape[1]
    for part in range(2):
        total = part_refs[0][part * rows : (part + 1) * rows].astype(jnp.float32)
        for ref in part_refs[1:]:
            total += ref[part * rows : (part + 1) * rows].astype(jnp.float32)
        rounded = total.astype(jnp.bfloat16)
        if keep_ahead:
            beams_ref[part] = rounded[:edge]
        wide_ref[part, :rows] = rounded.astype(jnp.float32)
        if halo:
            wide_ref[part, rows:] = ahead_ref[part].astype(jnp.float32)
        else:
            wide_ref[part, rows:] = jnp.zeros((edge, lanes), jnp.float32)
    lens, limits = lens_ref[...], limits_ref[...]
    pulse = at_ref[0] + lax.broadcasted_iota(jnp.int32, (pulses, lanes), 0)
    keep = pulse < limits
    factors = [
        (jnp.where(tap < lens, code_ref[0, tap], 0.0), jnp.where(tap < lens, code_ref[1, tap], 0.0))
        for tap in range(taps)
    ]
    for gate in range(rows // pulses):
        real = imag = None
        for tap, (code_re, code_im) in enumerate(factors):
            start = (gate + tap) * pulses
            shift_re = wide_ref[0, start : start + pulses]
            shift_im = wide_ref[1, start : start + pulses]
            term_re = code_re * shift_re + code_im * shift_im
            term_im = code_re * shift_im - code_im * shift_re
            real = term_re if real is None else real + term_re
            imag = term_im if imag is None else imag + term_im
        real = jnp.where(keep, real, 0.0)
        imag = jnp.where(keep, imag, 0.0)
        for owner in range(lanes // own):
            block = jnp.concatenate(
                [real[:, owner * own : (owner + 1) * own], imag[:, owner * own : (owner + 1) * own]], axis=1
            )
            out_ref[owner, gate * pulses : (gate + 1) * pulses] = block.astype(jnp.bfloat16)


def compress(parts, ahead, code, at, lens, limits, pulses, owners, keep_ahead):
    taps = code.shape[1]
    rows, tile_beams = parts[0].shape[0] // 2, parts[0].shape[1]
    own = tile_beams // owners
    lanes = block_of(tile_beams, 256)
    edge = (taps - 1) * pulses
    flat = pl.BlockSpec((2 * rows, lanes), lambda i: (0, i))
    line = pl.BlockSpec((1, lanes), lambda i: (0, i))
    edges = pl.BlockSpec((2, edge, lanes), lambda i: (0, 0, i))
    scalars = pl.BlockSpec(memory_space=pltpu.SMEM)
    out_specs = [pl.BlockSpec((lanes // own, rows, 2 * own), lambda i: (i, 0, 0))]
    out_shape = [jax.ShapeDtypeStruct((owners, rows, 2 * own), jnp.bfloat16)]
    if keep_ahead:
        out_specs.append(edges)
        out_shape.append(jax.ShapeDtypeStruct((2, edge, tile_beams), jnp.bfloat16))
    halo = [] if ahead is None else [ahead]
    done = pl.pallas_call(
        functools.partial(compress_kernel, pulses, taps, len(parts), len(halo), keep_ahead, own),
        grid=(tile_beams // lanes,),
        in_specs=[scalars, scalars, line, line] + [flat] * len(parts) + [edges] * len(halo),
        out_specs=out_specs,
        out_shape=out_shape,
        scratch_shapes=[pltpu.VMEM((2, rows + edge, lanes), jnp.float32)],
        compiler_params=params(),
        cost_estimate=pl.CostEstimate(
            flops=rows * tile_beams * 8 * taps, bytes_accessed=rows * tile_beams * 12, transcendentals=0
        ),
        name="compress",
    )(code, at, lens, limits, *parts, *halo)
    return done if keep_ahead else (done[0], None)


def doppler_kernel(pulses, got_ref, table_ref, *rest):
    out_ref, lines_ref = rest[-2:]
    owners, rows, lanes = got_ref.shape
    own, bins = lanes // 2, table_ref.shape[1] // 2
    gates = rows // pulses
    for gate in range(gates):
        values = got_ref[:, gate * pulses : (gate + 1) * pulses].reshape(owners * pulses, lanes)
        both = lax.dot_general(values, table_ref[...], TN, preferred_element_type=jnp.float32)
        real = both[:own, :bins] - both[own:, bins:]
        imag = both[own:, :bins] + both[:own, bins:]
        for part, values in enumerate((real, imag)):
            for at in range(lines_ref.shape[0]):
                lines_ref[at, pl.ds(part * gates + gate, own, stride=2 * gates), :] = values[:, at * 128 : (at + 1) * 128]
    for at in range(lines_ref.shape[0]):
        out_ref[:, :, :, at * 128 : (at + 1) * 128] = lines_ref[at].reshape(own, 2, gates, 128)


def doppler(got, table, out, first, pulses):
    owners, rows, lanes = got.shape
    own, bins, gates = lanes // 2, table.shape[1] // 2, rows // pulses
    return pl.pallas_call(
        functools.partial(doppler_kernel, pulses),
        grid=(1,),
        in_specs=[
            pl.BlockSpec(got.shape, lambda i: (0, 0, 0)),
            pl.BlockSpec(table.shape, lambda i: (0, 0)),
        ]
        + ([] if out is None else [pl.BlockSpec(memory_space=pl.ANY)]),
        out_specs=pl.BlockSpec((own, 2, gates, bins), lambda i: (0, 0, first // gates, 0)),
        out_shape=jax.ShapeDtypeStruct((own, 2, G, bins), jnp.float32),
        scratch_shapes=[pltpu.VMEM((bins // 128, own * 2 * gates, 128), jnp.float32)],
        input_output_aliases={} if out is None else {2: 0},
        compiler_params=params(),
        cost_estimate=pl.CostEstimate(
            flops=rows * lanes * owners * bins * 4, bytes_accessed=got.size * 2 + own * 8 * gates * bins, transcendentals=0
        ),
        name="doppler",
    )(got, table, *([] if out is None else [out]))


def phase_table(total):
    angle = np.outer(np.arange(total), np.arange(total)) % total * (2.0 * math.pi / total)
    return np.concatenate([np.cos(angle), -np.sin(angle)], axis=1) / math.sqrt(total)


def sum_over(values, axis):
    size = lax.axis_size(axis)
    if size & (size - 1):
        return lax.psum(values, axis)
    step = 1
    while step < size:
        values = values + lax.ppermute(values, axis, [(i, i ^ step) for i in range(size)])
        step *= 2
    return values


def on_device(echoes, steer, code, beam_order, dwell, code_len):
    tiles, owners = lax.axis_size("tile"), lax.axis_size("beam")
    columns = echoes.shape[2]
    beam_total = steer.shape[1]
    pulses = columns // G
    total = pulses * owners
    tile_beams = beam_total // tiles
    own = tile_beams // owners

    turned, local = prep(echoes, G)
    power = sum_over(local, "beam")

    mine = lax.axis_index("tile")
    order = jnp.roll(beam_order, -mine * tile_beams)
    here = order[:tile_beams]
    match = jnp.arange(beam_total, dtype=jnp.int32)[:, None] == here[None, :]
    both = jnp.sum(jnp.where(match, (dwell * 16 + code_len)[:, None], 0), axis=0)
    lens, limits = (both % 16)[None, :], (both // 16)[None, :]
    at = (lax.axis_index("beam") * pulses)[None]
    taps = code.astype(jnp.float32)
    table = jnp.asarray(phase_table(total).astype(jnp.bfloat16))

    out = ahead = None
    chunks = chunks_of(G)
    for number, (gate, gates) in enumerate(chunks):
        with jax.named_scope("beams"):
            parts = form_beams(
                turned, power, order[None, :], steer, gate * pulses, gates * pulses, total * G, tiles
            )
        with jax.named_scope("tile_sum"):
            parts = [parts[0]] + [
                lax.ppermute(part, "tile", [(i, (i + away) % tiles) for i in range(tiles)])
                for away, part in enumerate(parts[1:], 1)
            ]
        with jax.named_scope("compress"):
            ready, ahead = compress(
                parts, ahead, taps, at, lens, limits, pulses, owners, number < len(chunks) - 1
            )
        with jax.named_scope("to_owners"):
            got = lax.all_to_all(ready, "beam", split_axis=0, concat_axis=0)
        with jax.named_scope("doppler"):
            out = doppler(got, table, out, gate, pulses)
    return out


def solution(mesh):
    placed = (P(None, "tile", "beam"), P(None, None, "tile"), P(), P(), P(), P())
    return jax.shard_map(
        on_device,
        mesh=mesh,
        in_specs=placed,
        out_specs=P(("tile", "beam"), None, None, None),
        check_vma=False,
    )
```

```python
import functools
import math

import jax
import jax.numpy as jnp
import numpy as np
from jax import lax
from jax.experimental import pallas as pl
from jax.experimental.pallas import tpu as pltpu
from jax.sharding import PartitionSpec as P

G = 32
EPS = 1e-05
CHUNK = 8
TOGETHER = (2, 2)
NT = (((1,), (1,)), ((), ()))
TN = (((0,), (0,)), ((), ()))
MIB = 1024 * 1024


def params(mib):
    return pltpu.CompilerParams(vmem_limit_bytes=mib * MIB)


def block_of(size, most):
    return max(n for n in range(1, min(size, most) + 1) if size % n == 0)


def groups_of(gates):
    if CHUNK * sum(TOGETHER) != gates:
        return [[(0, gates)]]
    found, end = [], gates
    for count in TOGETHER:
        found.append([(end - CHUNK * (i + 1), CHUNK) for i in range(count)])
        end -= CHUNK * count
    return found


def in_hbm(*values):
    return [pltpu.with_memory_space_constraint(x, pltpu.HBM) for x in values]


def beam_kernel(samples, gates, gate, count, echoes_hbm, power_ref, order_ref, steer_hbm, *rest):
    out_refs = rest[:-7]
    echoes_ref, steer_ref, scaled_ref, row_ref, picked_ref, echoes_sem, steer_sem = rest[-7:]
    _, chans, columns = echoes_ref.shape
    beam_total, wide = steer_ref.shape[1], row_ref.shape[0]
    pulses = columns // gates
    rows = count * pulses

    def echoes_copy(part):
        return pltpu.make_async_copy(echoes_hbm.at[part], echoes_ref.at[part], echoes_sem.at[part])

    def steer_copy(part, step):
        at = pl.ds(step * wide, wide)
        return pltpu.make_async_copy(
            steer_hbm.at[part, at], steer_ref.at[part, at], steer_sem.at[part, step]
        )

    def begin(step):
        for part in range(2):
            steer_copy(part, step).start()

    steps = beam_total // wide
    for part in range(2):
        echoes_copy(part).start()
    begin(0)
    row = lax.broadcasted_iota(jnp.int32, (rows, columns), 0)
    col = lax.broadcasted_iota(jnp.int32, (rows, columns), 1)
    source = (row % pulses) * gates + row // pulses + gate
    moved = jnp.where(source == col, 1.0, 0.0).astype(jnp.bfloat16)
    row_ref[...] = lax.broadcasted_iota(jnp.int32, row_ref.shape, 0)
    gain = lax.rsqrt(power_ref[...] / samples + EPS)
    for part in range(2):
        echoes_copy(part).wait()
        if part == 0 and steps > 1:
            begin(1)
        turned = lax.dot_general(moved, echoes_ref[part], NT, preferred_element_type=jnp.float32) * gain
        if part == 0:
            scaled_ref[:rows, :chans] = turned.astype(jnp.bfloat16)
            scaled_ref[rows:, chans:] = turned.astype(jnp.bfloat16)
        else:
            scaled_ref[:rows, chans:] = (-turned).astype(jnp.bfloat16)
            scaled_ref[rows:, :chans] = turned.astype(jnp.bfloat16)

    slots = row_ref.shape[1]
    for step in range(steps):
        at = slice(step * wide, (step + 1) * wide)
        for part in range(2):
            steer_copy(part, step).wait()
        if step + 2 < steps:
            begin(step + 2)
        beams = lax.dot_general(scaled_ref[:, :chans], steer_ref[0, at], NT, preferred_element_type=jnp.float32)
        beams += lax.dot_general(scaled_ref[:, chans:], steer_ref[1, at], NT, preferred_element_type=jnp.float32)
        beams = beams.astype(jnp.bfloat16)
        for start in range(0, beam_total, slots):
            wanted = order_ref[:, start : start + slots] - step * wide
            pick = jnp.where(row_ref[...] == wanted, 1.0, 0.0).astype(jnp.bfloat16)
            picked = jnp.dot(beams, pick, preferred_element_type=jnp.float32)
            if step > 0:
                picked += picked_ref[:, start : start + slots]
            picked_ref[:, start : start + slots] = picked

    for index, out_ref in enumerate(out_refs):
        slots = out_ref.shape[1]
        out_ref[...] = picked_ref[:, index * slots : (index + 1) * slots].astype(jnp.bfloat16)


def form_beams(echoes, power, order, steer, gates, gate, count, samples, tiles):
    _, chans, columns = echoes.shape
    beam_total = steer.shape[1]
    tile_beams = beam_total // tiles
    rows = columns // gates * count
    wide = block_of(beam_total, 512)
    echoes, steer = in_hbm(echoes, steer)
    whole = pl.BlockSpec(memory_space=pltpu.VMEM)
    apart = pl.BlockSpec(memory_space=pl.ANY)
    return pl.pallas_call(
        functools.partial(beam_kernel, samples, gates, gate, count),
        in_specs=[apart, whole, whole, apart],
        out_specs=[whole] * tiles,
        out_shape=[pltpu.HBM((2 * rows, tile_beams), jnp.bfloat16)] * tiles,
        scratch_shapes=[
            pltpu.VMEM(echoes.shape, jnp.bfloat16),
            pltpu.VMEM(steer.shape, jnp.bfloat16),
            pltpu.VMEM((2 * rows, 2 * chans), jnp.bfloat16),
            pltpu.VMEM((wide, block_of(beam_total, 512)), jnp.int32),
            pltpu.VMEM((2 * rows, beam_total), jnp.float32),
            pltpu.SemaphoreType.DMA((2,)),
            pltpu.SemaphoreType.DMA((2, beam_total // wide)),
        ],
        compiler_params=params(40),
        cost_estimate=pl.CostEstimate(
            flops=4 * rows * beam_total * (2 * chans + beam_total),
            bytes_accessed=steer.size * 2 + 4 * rows * beam_total,
            transcendentals=0,
        ),
        name="beams",
    )(echoes, power, order, steer)


def compress_kernel(pulses, taps, parts_in, halo, shared, keep_ahead, own, code_ref, at_ref, lens_ref, limits_ref, *rest):
    part_refs, rest = rest[:parts_in], rest[parts_in:]
    if halo:
        ahead_ref, rest = rest[0], rest[1:]
    out_ref, rest = rest[shared], rest[shared + 1 :]
    if keep_ahead:
        beams_ref, rest = rest[0], rest[1:]
    (wide_ref,) = rest
    rows = part_refs[0].shape[0] // 2
    edge = (taps - 1) * pulses
    lanes = part_refs[0].shape[1]
    for part in range(2):
        total = part_refs[0][part * rows : (part + 1) * rows].astype(jnp.float32)
        for ref in part_refs[1:]:
            total += ref[part * rows : (part + 1) * rows].astype(jnp.float32)
        rounded = total.astype(jnp.bfloat16)
        if keep_ahead:
            beams_ref[part] = rounded[:edge]
        wide_ref[part, :rows] = rounded.astype(jnp.float32)
        if halo:
            wide_ref[part, rows:] = ahead_ref[part].astype(jnp.float32)
        else:
            wide_ref[part, rows:] = jnp.zeros((edge, lanes), jnp.float32)
    lens, limits = lens_ref[...], limits_ref[...]
    pulse = at_ref[0] + lax.broadcasted_iota(jnp.int32, (pulses, lanes), 0)
    keep = pulse < limits
    factors = [
        (jnp.where(tap < lens, code_ref[0, tap], 0.0), jnp.where(tap < lens, code_ref[1, tap], 0.0))
        for tap in range(taps)
    ]
    for gate in range(rows // pulses):
        real = imag = None
        for tap, (code_re, code_im) in enumerate(factors):
            start = (gate + tap) * pulses
            shift_re = wide_ref[0, start : start + pulses]
            shift_im = wide_ref[1, start : start + pulses]
            term_re = code_re * shift_re + code_im * shift_im
            term_im = code_re * shift_im - code_im * shift_re
            real = term_re if real is None else real + term_re
            imag = term_im if imag is None else imag + term_im
        real = jnp.where(keep, real, 0.0)
        imag = jnp.where(keep, imag, 0.0)
        for owner in range(lanes // own):
            block = jnp.concatenate(
                [real[:, owner * own : (owner + 1) * own], imag[:, owner * own : (owner + 1) * own]], axis=1
            )
            out_ref[owner, gate * pulses : (gate + 1) * pulses] = block.astype(jnp.bfloat16)


def compress(parts, ahead, code, at, lens, limits, pulses, owners, keep_ahead, ready, place, places):
    taps = code.shape[1]
    rows, tile_beams = parts[0].shape[0] // 2, parts[0].shape[1]
    own = tile_beams // owners
    lanes = block_of(tile_beams, 256)
    edge = (taps - 1) * pulses
    flat = pl.BlockSpec((2 * rows, lanes), lambda i: (0, i))
    line = pl.BlockSpec((1, lanes), lambda i: (0, i))
    edges = pl.BlockSpec((2, edge, lanes), lambda i: (0, 0, i))
    scalars = pl.BlockSpec(memory_space=pltpu.SMEM)
    out_specs = [pl.BlockSpec((lanes // own, rows, 2 * own), lambda i: (i, place, 0))]
    out_shape = [pltpu.HBM((owners, places * rows, 2 * own), jnp.bfloat16)]
    if keep_ahead:
        out_specs.append(edges)
        out_shape.append(pltpu.HBM((2, edge, tile_beams), jnp.bfloat16))
    halo = [] if ahead is None else [ahead]
    shared = [] if ready is None else [ready]
    done = pl.pallas_call(
        functools.partial(compress_kernel, pulses, taps, len(parts), len(halo), len(shared), keep_ahead, own),
        grid=(tile_beams // lanes,),
        in_specs=[scalars, scalars, line, line] + [flat] * len(parts)
        + [edges] * len(halo)
        + [pl.BlockSpec(memory_space=pl.ANY)] * len(shared),
        out_specs=out_specs,
        out_shape=out_shape,
        scratch_shapes=[pltpu.VMEM((2, rows + edge, lanes), jnp.float32)],
        input_output_aliases={4 + len(parts) + len(halo): 0} if shared else {},
        compiler_params=params(16),
        cost_estimate=pl.CostEstimate(
            flops=rows * tile_beams * 8 * taps, bytes_accessed=rows * tile_beams * 12, transcendentals=0
        ),
        name="compress",
    )(code, at, lens, limits, *parts, *halo, *shared)
    return done if keep_ahead else (done[0], None)


def doppler_kernel(pulses, got_ref, table_ref, *rest):
    out_ref, lines_ref = rest[-2:]
    owners, rows, lanes = got_ref.shape
    own, bins = lanes // 2, table_ref.shape[1] // 2
    gates = rows // pulses
    for gate in range(gates):
        values = got_ref[:, gate * pulses : (gate + 1) * pulses].reshape(owners * pulses, lanes)
        both = lax.dot_general(values, table_ref[...], TN, preferred_element_type=jnp.float32)
        real = both[:own, :bins] - both[own:, bins:]
        imag = both[own:, :bins] + both[:own, bins:]
        for part, values in enumerate((real, imag)):
            for at in range(lines_ref.shape[0]):
                lines_ref[at, pl.ds(part * gates + gate, own, stride=2 * gates), :] = values[:, at * 128 : (at + 1) * 128]
    for at in range(lines_ref.shape[0]):
        out_ref[:, :, :, at * 128 : (at + 1) * 128] = lines_ref[at].reshape(own, 2, gates, 128)


def doppler(got, table, out, first, pulses):
    owners, rows, lanes = got.shape
    own, bins, gates = lanes // 2, table.shape[1] // 2, rows // pulses
    return pl.pallas_call(
        functools.partial(doppler_kernel, pulses),
        grid=(1,),
        in_specs=[
            pl.BlockSpec(got.shape, lambda i: (0, 0, 0)),
            pl.BlockSpec(table.shape, lambda i: (0, 0)),
        ]
        + ([] if out is None else [pl.BlockSpec(memory_space=pl.ANY)]),
        out_specs=pl.BlockSpec((own, 2, gates, bins), lambda i: (0, 0, first // gates, 0)),
        out_shape=jax.ShapeDtypeStruct((own, 2, G, bins), jnp.float32),
        scratch_shapes=[pltpu.VMEM((bins // 128, own * 2 * gates, 128), jnp.float32)],
        input_output_aliases={} if out is None else {2: 0},
        compiler_params=params(24),
        cost_estimate=pl.CostEstimate(
            flops=rows * lanes * owners * bins * 4, bytes_accessed=got.size * 2 + own * 8 * gates * bins, transcendentals=0
        ),
        name="doppler",
    )(got, table, *([] if out is None else [out]))


def phase_table(total):
    angle = np.outer(np.arange(total), np.arange(total)) % total * (2.0 * math.pi / total)
    return np.concatenate([np.cos(angle), -np.sin(angle)], axis=1) / math.sqrt(total)


def sum_over(values, axis):
    size = lax.axis_size(axis)
    if size & (size - 1):
        return lax.psum(values, axis)
    step = 1
    while step < size:
        steps = [step * i for i in (1, 2, 3) if step * i < size] if step * 2 < size else [step]
        values = values + sum(
            lax.ppermute(values, axis, [(i, i ^ away) for i in range(size)]) for away in steps
        )
        step *= len(steps) + 1
    return values


def order_of(groups):
    count = sum(len(group) for group in groups)
    if count == 1:
        return [("beams", 0), ("compress", 0), ("send", 0), ("doppler", 0)]
    return [
        ("beams", 0),
        ("beams<beams", 0),
        ("beams", 1),
        ("beams<compress", (1, 0)),
        ("compress", 0),
        ("compress<beams", 0),
        ("beams", 2),
        ("beams<compress", (2, 1)),
        ("compress", 1),
        ("compress<beams", 1),
        ("send", 0),
        ("beams", 3),
        ("beams<compress", (3, 2)),
        ("compress", 2),
        ("compress", 3),
        ("send", 1),
        ("doppler", 0),
        ("doppler", 1),
    ]


def on_device(echoes, steer, code, beam_order, dwell, code_len):
    tiles, owners = lax.axis_size("tile"), lax.axis_size("beam")
    columns = echoes.shape[2]
    beam_total = steer.shape[1]
    pulses = columns // G
    total = pulses * owners
    tile_beams = beam_total // tiles
    own = tile_beams // owners

    values = echoes.astype(jnp.float32)
    power = sum_over(jnp.sum(values * values, axis=(0, 2))[None, :], "beam")

    mine = lax.axis_index("tile")
    order = jnp.roll(beam_order, -mine * tile_beams)
    here = order[:tile_beams]
    match = jnp.arange(beam_total, dtype=jnp.int32)[:, None] == here[None, :]
    both = jnp.sum(jnp.where(match, (dwell * 16 + code_len)[:, None], 0), axis=0)
    lens, limits = (both % 16)[None, :], (both // 16)[None, :]
    at = (lax.axis_index("beam") * pulses)[None]
    taps = code.astype(jnp.float32)
    table = jnp.asarray(phase_table(total).astype(jnp.bfloat16))

    groups = groups_of(G)
    chunks = [chunk for group in groups for chunk in group]
    owner_of = [index for index, group in enumerate(groups) for _ in group]
    firsts = [owner_of.index(index) for index in range(len(groups))]
    own_parts, others, ready, ahead, got, out = {}, {}, {}, {}, {}, None
    for kind, number in order_of(groups):
        if kind == "beams":
            gate, gates = chunks[number]
            with jax.named_scope("beams"):
                parts = form_beams(
                    echoes, power, order[None, :], steer, G, gate, gates, total * G, tiles
                )
            own_parts[number] = parts[0]
            with jax.named_scope("tile_sum"):
                others[number] = [
                    lax.ppermute(part, "tile", [(i, (i + away) % tiles) for i in range(tiles)])
                    for away, part in enumerate(parts[1:], 1)
                ]
        elif kind == "compress":
            index = owner_of[number]
            place = number - firsts[index]
            with jax.named_scope("compress"):
                ready[index], ahead[number] = compress(
                    [own_parts[number]] + others[number],
                    ahead.get(number - 1), taps, at, lens, limits, pulses, owners, number < len(chunks) - 1,
                    ready.get(index), len(groups[index]) - 1 - place, len(groups[index]),
                )
        elif kind == "send":
            with jax.named_scope("to_owners"):
                got[number] = lax.all_to_all(ready[number], "beam", split_axis=0, concat_axis=0)
        elif kind == "doppler":
            with jax.named_scope("doppler"):
                out = doppler(got[number], table, out, groups[number][-1][0], pulses)
        elif kind == "beams<beams":
            power, own_parts[number] = lax.optimization_barrier((power, own_parts[number]))
        elif kind == "beams<compress":
            own_parts[number[1]], own_parts[number[0]] = lax.optimization_barrier(
                (own_parts[number[1]], own_parts[number[0]])
            )
        elif kind == "arrived<beams":
            power, others[number][0] = lax.optimization_barrier((power, others[number][0]))
        elif kind == "arrived<doppler":
            table, others[number][0] = lax.optimization_barrier((table, others[number][0]))
        elif kind == "compress<beams":
            index = owner_of[number]
            power, ready[index] = lax.optimization_barrier((power, ready[index]))
        elif kind == "compress<doppler":
            table, ahead[number] = lax.optimization_barrier((table, ahead[number]))
        elif kind == "doppler<compress":
            ahead[number], out = lax.optimization_barrier((ahead[number], out))
        elif kind == "last<doppler":
            out, ready[number] = lax.optimization_barrier((out, ready[number]))
    return out


def solution(mesh):
    placed = (P(None, "tile", "beam"), P(None, None, "tile"), P(), P(), P(), P())
    return jax.shard_map(
        on_device,
        mesh=mesh,
        in_specs=placed,
        out_specs=P(("tile", "beam"), None, None, None),
        check_vma=False,
    )
```

```python
import functools
import math

import jax
import jax.numpy as jnp
import numpy as np
from jax import lax
from jax.experimental import pallas as pl
from jax.experimental.pallas import tpu as pltpu
from jax.sharding import PartitionSpec as P

G = 32
EPS = 1e-05
CHUNK = 8
TOGETHER = (2, 2)
NT = (((1,), (1,)), ((), ()))
TN = (((0,), (0,)), ((), ()))
MIB = 1024 * 1024


def params(mib):
    return pltpu.CompilerParams(vmem_limit_bytes=mib * MIB)


def block_of(size, most):
    return max(n for n in range(1, min(size, most) + 1) if size % n == 0)


def groups_of(gates):
    if CHUNK * sum(TOGETHER) != gates:
        return [[(0, gates)]]
    found, end = [], gates
    for count in TOGETHER:
        found.append([(end - CHUNK * (i + 1), CHUNK) for i in range(count)])
        end -= CHUNK * count
    return found


def in_hbm(*values):
    return [pltpu.with_memory_space_constraint(x, pltpu.HBM) for x in values]


def beam_kernel(samples, gates, gate, count, echoes_hbm, power_ref, order_ref, steer_hbm, *rest):
    out_refs = rest[:-7]
    echoes_ref, steer_ref, scaled_ref, row_ref, picked_ref, echoes_sem, steer_sem = rest[-7:]
    _, chans, columns = echoes_ref.shape
    beam_total, wide = steer_ref.shape[1], row_ref.shape[0]
    pulses = columns // gates
    rows = count * pulses

    def echoes_copy(part):
        return pltpu.make_async_copy(echoes_hbm.at[part], echoes_ref.at[part], echoes_sem.at[part])

    def steer_copy(part, step):
        at = pl.ds(step * wide, wide)
        return pltpu.make_async_copy(
            steer_hbm.at[part, at], steer_ref.at[part, at], steer_sem.at[part, step]
        )

    def begin(step):
        for part in range(2):
            steer_copy(part, step).start()

    steps = beam_total // wide
    for part in range(2):
        echoes_copy(part).start()
    begin(0)
    row = lax.broadcasted_iota(jnp.int32, (rows, columns), 0)
    col = lax.broadcasted_iota(jnp.int32, (rows, columns), 1)
    source = (row % pulses) * gates + row // pulses + gate
    moved = jnp.where(source == col, 1.0, 0.0).astype(jnp.bfloat16)
    row_ref[...] = lax.broadcasted_iota(jnp.int32, row_ref.shape, 0)
    gain = lax.rsqrt(power_ref[...] / samples + EPS)
    for part in range(2):
        echoes_copy(part).wait()
        if part == 0 and steps > 1:
            begin(1)
        turned = lax.dot_general(moved, echoes_ref[part], NT, preferred_element_type=jnp.float32) * gain
        if part == 0:
            scaled_ref[:rows, :chans] = turned.astype(jnp.bfloat16)
            scaled_ref[rows:, chans:] = turned.astype(jnp.bfloat16)
        else:
            scaled_ref[:rows, chans:] = (-turned).astype(jnp.bfloat16)
            scaled_ref[rows:, :chans] = turned.astype(jnp.bfloat16)

    slots = row_ref.shape[1]
    for step in range(steps):
        at = slice(step * wide, (step + 1) * wide)
        for part in range(2):
            steer_copy(part, step).wait()
        if step + 2 < steps:
            begin(step + 2)
        beams = lax.dot_general(scaled_ref[:, :chans], steer_ref[0, at], NT, preferred_element_type=jnp.float32)
        beams += lax.dot_general(scaled_ref[:, chans:], steer_ref[1, at], NT, preferred_element_type=jnp.float32)
        beams = beams.astype(jnp.bfloat16)
        for start in range(0, beam_total, slots):
            wanted = order_ref[:, start : start + slots] - step * wide
            pick = jnp.where(row_ref[...] == wanted, 1.0, 0.0).astype(jnp.bfloat16)
            picked = jnp.dot(beams, pick, preferred_element_type=jnp.float32)
            if step > 0:
                picked += picked_ref[:, start : start + slots]
            picked_ref[:, start : start + slots] = picked

    for index, out_ref in enumerate(out_refs):
        slots = out_ref.shape[1]
        out_ref[...] = picked_ref[:, index * slots : (index + 1) * slots].astype(jnp.bfloat16)


def form_beams(echoes, power, order, steer, gates, gate, count, samples, tiles):
    _, chans, columns = echoes.shape
    beam_total = steer.shape[1]
    tile_beams = beam_total // tiles
    rows = columns // gates * count
    wide = block_of(beam_total, 512)
    echoes, steer = in_hbm(echoes, steer)
    whole = pl.BlockSpec(memory_space=pltpu.VMEM)
    apart = pl.BlockSpec(memory_space=pl.ANY)
    return pl.pallas_call(
        functools.partial(beam_kernel, samples, gates, gate, count),
        in_specs=[apart, whole, whole, apart],
        out_specs=[whole] * tiles,
        out_shape=[pltpu.VMEM((2 * rows, tile_beams), jnp.bfloat16)]
        + [pltpu.HBM((2 * rows, tile_beams), jnp.bfloat16)] * (tiles - 1),
        scratch_shapes=[
            pltpu.VMEM(echoes.shape, jnp.bfloat16),
            pltpu.VMEM(steer.shape, jnp.bfloat16),
            pltpu.VMEM((2 * rows, 2 * chans), jnp.bfloat16),
            pltpu.VMEM((wide, block_of(beam_total, 512)), jnp.int32),
            pltpu.VMEM((2 * rows, beam_total), jnp.float32),
            pltpu.SemaphoreType.DMA((2,)),
            pltpu.SemaphoreType.DMA((2, beam_total // wide)),
        ],
        compiler_params=params(40),
        cost_estimate=pl.CostEstimate(
            flops=4 * rows * beam_total * (2 * chans + beam_total),
            bytes_accessed=steer.size * 2 + 4 * rows * beam_total,
            transcendentals=0,
        ),
        name="beams",
    )(echoes, power, order, steer)


def compress_kernel(pulses, taps, parts_in, halo, shared, keep_ahead, place, code_ref, at_ref, lens_ref, limits_ref, *rest):
    part_refs, rest = rest[:parts_in], rest[parts_in:]
    if halo:
        ahead_ref, rest = rest[0], rest[1:]
    out_hbm, rest = rest[shared], rest[shared + 1 :]
    if keep_ahead:
        beams_ref, rest = rest[0], rest[1:]
    wide_ref, laid_ref, sem = rest
    rows, tile_beams = part_refs[0].shape[0] // 2, part_refs[0].shape[1]
    edge = (taps - 1) * pulses
    lanes = wide_ref.shape[2]
    own = laid_ref.shape[2] // 2
    some = lanes // own

    def copy(block):
        at = pl.ds(block * some, some)
        return pltpu.make_async_copy(
            laid_ref.at[at], out_hbm.at[at, pl.ds(place * rows, rows)], sem.at[block]
        )

    for block in range(tile_beams // lanes):
        at = slice(block * lanes, (block + 1) * lanes)
        for part in range(2):
            total = part_refs[0][part * rows : (part + 1) * rows, at].astype(jnp.float32)
            for ref in part_refs[1:]:
                total += ref[part * rows : (part + 1) * rows, at].astype(jnp.float32)
            rounded = total.astype(jnp.bfloat16)
            if keep_ahead:
                beams_ref[part, :, at] = rounded[:edge]
            wide_ref[part, :rows] = rounded.astype(jnp.float32)
            if halo:
                wide_ref[part, rows:] = ahead_ref[part, :, at].astype(jnp.float32)
            else:
                wide_ref[part, rows:] = jnp.zeros((edge, lanes), jnp.float32)
        lens, limits = lens_ref[:, at], limits_ref[:, at]
        pulse = at_ref[0] + lax.broadcasted_iota(jnp.int32, (pulses, lanes), 0)
        keep = pulse < limits
        factors = [
            (jnp.where(tap < lens, code_ref[0, tap], 0.0), jnp.where(tap < lens, code_ref[1, tap], 0.0))
            for tap in range(taps)
        ]
        for gate in range(rows // pulses):
            real = imag = None
            for tap, (code_re, code_im) in enumerate(factors):
                start = (gate + tap) * pulses
                shift_re = wide_ref[0, start : start + pulses]
                shift_im = wide_ref[1, start : start + pulses]
                term_re = code_re * shift_re + code_im * shift_im
                term_im = code_re * shift_im - code_im * shift_re
                real = term_re if real is None else real + term_re
                imag = term_im if imag is None else imag + term_im
            real = jnp.where(keep, real, 0.0)
            imag = jnp.where(keep, imag, 0.0)
            for owner in range(some):
                line = slice(owner * own, (owner + 1) * own)
                joined = jnp.concatenate([real[:, line], imag[:, line]], axis=1).astype(jnp.bfloat16)
                laid_ref[block * some + owner, gate * pulses : (gate + 1) * pulses] = joined
        copy(block).start()
    for block in range(tile_beams // lanes):
        copy(block).wait()


def compress(parts, ahead, code, at, lens, limits, pulses, owners, keep_ahead, ready, place, places):
    taps = code.shape[1]
    rows, tile_beams = parts[0].shape[0] // 2, parts[0].shape[1]
    own = tile_beams // owners
    lanes = block_of(tile_beams, 256)
    edge = (taps - 1) * pulses
    whole, apart = pl.BlockSpec(memory_space=pltpu.VMEM), pl.BlockSpec(memory_space=pl.ANY)
    scalars = pl.BlockSpec(memory_space=pltpu.SMEM)
    out_shape = [pltpu.HBM((owners, places * rows, 2 * own), jnp.bfloat16)]
    if keep_ahead:
        out_shape.append(pltpu.VMEM((2, edge, tile_beams), jnp.bfloat16))
    near = [pltpu.with_memory_space_constraint(x, pltpu.VMEM) for x in parts + ([] if ahead is None else [ahead])]
    shared = [] if ready is None else in_hbm(ready)
    done = pl.pallas_call(
        functools.partial(
            compress_kernel, pulses, taps, len(parts), ahead is not None, len(shared), keep_ahead, place
        ),
        in_specs=[scalars, scalars, whole, whole] + [whole] * len(near) + [apart] * len(shared),
        out_specs=[apart] + [whole] * keep_ahead,
        out_shape=out_shape,
        scratch_shapes=[
            pltpu.VMEM((2, rows + edge, lanes), jnp.float32),
            pltpu.VMEM((owners, rows, 2 * own), jnp.bfloat16),
            pltpu.SemaphoreType.DMA((tile_beams // lanes,)),
        ],
        input_output_aliases={4 + len(near): 0} if shared else {},
        compiler_params=params(16),
        name="compress",
    )(code, at, lens, limits, *near, *shared)
    return done if keep_ahead else (done[0], None)


def doppler_kernel(pulses, got_ref, table_ref, *rest):
    out_ref, lines_ref = rest[-2:]
    owners, rows, lanes = got_ref.shape
    own, bins = lanes // 2, table_ref.shape[1] // 2
    gates = rows // pulses
    some = block_of(gates, max(1, 512 // lanes))
    for first in range(0, gates, some):
        values = jnp.concatenate(
            [
                got_ref[:, gate * pulses : (gate + 1) * pulses].reshape(owners * pulses, lanes)
                for gate in range(first, first + some)
            ],
            axis=1,
        )
        both = lax.dot_general(values, table_ref[...], TN, preferred_element_type=jnp.float32)
        for index in range(some):
            gate, start = first + index, index * lanes
            upper, lower = both[start : start + own], both[start + own : start + lanes]
            real = upper[:, :bins] - lower[:, bins:]
            imag = lower[:, :bins] + upper[:, bins:]
            for part, line in enumerate((real, imag)):
                for at in range(lines_ref.shape[0]):
                    lines_ref[at, pl.ds(part * gates + gate, own, stride=2 * gates), :] = line[
                        :, at * 128 : (at + 1) * 128
                    ]
    for at in range(lines_ref.shape[0]):
        out_ref[:, :, :, at * 128 : (at + 1) * 128] = lines_ref[at].reshape(own, 2, gates, 128)


def doppler(got, table, out, first, pulses):
    owners, rows, lanes = got.shape
    own, bins, gates = lanes // 2, table.shape[1] // 2, rows // pulses
    some = CHUNK if gates % CHUNK == 0 else gates
    return pl.pallas_call(
        functools.partial(doppler_kernel, pulses),
        grid=(gates // some,),
        in_specs=[
            pl.BlockSpec((owners, some * pulses, lanes), lambda i: (0, i, 0)),
            pl.BlockSpec(table.shape, lambda i: (0, 0)),
        ]
        + ([] if out is None else [pl.BlockSpec(memory_space=pl.ANY)]),
        out_specs=pl.BlockSpec((own, 2, some, bins), lambda i: (0, 0, first // some + i, 0)),
        out_shape=jax.ShapeDtypeStruct((own, 2, G, bins), jnp.float32),
        scratch_shapes=[pltpu.VMEM((bins // 128, own * 2 * some, 128), jnp.float32)],
        input_output_aliases={} if out is None else {2: 0},
        compiler_params=params(24),
        name="doppler",
    )(got, table, *([] if out is None else [out]))


def phase_table(total):
    angle = np.outer(np.arange(total), np.arange(total)) % total * (2.0 * math.pi / total)
    return np.concatenate([np.cos(angle), -np.sin(angle)], axis=1) / math.sqrt(total)


def sum_over(values, axis):
    size = lax.axis_size(axis)
    if size & (size - 1):
        return lax.psum(values, axis)
    step = 1
    while step < size:
        steps = [step * i for i in (1, 2, 3) if step * i < size] if step * 2 < size else [step]
        values = values + sum(
            lax.ppermute(values, axis, [(i, i ^ away) for i in range(size)]) for away in steps
        )
        step *= len(steps) + 1
    return values


def order_of(groups):
    count = sum(len(group) for group in groups)
    if count == 1:
        return [("beams", 0), ("compress", 0), ("send", 0), ("doppler", 0)]
    return [
        ("beams", 0),
        ("beams<beams", 0),
        ("beams", 1),
        ("beams<beams", 1),
        ("beams", 2),
        ("beams<compress", (2, 0)),
        ("compress", 0),
        ("compress", 1),
        ("compress<beams", 1),
        ("send", 0),
        ("beams", 3),
        ("beams<compress", (3, 2)),
        ("compress", 2),
        ("compress", 3),
        ("send", 1),
        ("doppler", 0),
        ("doppler", 1),
    ]


def on_device(echoes, steer, code, beam_order, dwell, code_len):
    tiles, owners = lax.axis_size("tile"), lax.axis_size("beam")
    columns = echoes.shape[2]
    beam_total = steer.shape[1]
    pulses = columns // G
    total = pulses * owners
    tile_beams = beam_total // tiles
    own = tile_beams // owners

    values = echoes.astype(jnp.float32)
    power = sum_over(jnp.sum(values * values, axis=(0, 2))[None, :], "beam")

    mine = lax.axis_index("tile")
    order = jnp.roll(beam_order, -mine * tile_beams)
    here = order[:tile_beams]
    match = jnp.arange(beam_total, dtype=jnp.int32)[:, None] == here[None, :]
    both = jnp.sum(jnp.where(match, (dwell * 16 + code_len)[:, None], 0), axis=0)
    lens, limits = (both % 16)[None, :], (both // 16)[None, :]
    at = (lax.axis_index("beam") * pulses)[None]
    taps = code.astype(jnp.float32)
    table = jnp.asarray(phase_table(total).astype(jnp.bfloat16))

    groups = groups_of(G)
    chunks = [chunk for group in groups for chunk in group]
    owner_of = [index for index, group in enumerate(groups) for _ in group]
    firsts = [owner_of.index(index) for index in range(len(groups))]
    own_parts, others, ready, ahead, got, out = {}, {}, {}, {}, {}, None
    for kind, number in order_of(groups):
        if kind == "beams":
            gate, gates = chunks[number]
            with jax.named_scope("beams"):
                parts = form_beams(
                    echoes, power, order[None, :], steer, G, gate, gates, total * G, tiles
                )
            own_parts[number] = parts[0]
            with jax.named_scope("tile_sum"):
                others[number] = [
                    lax.ppermute(part, "tile", [(i, (i + away) % tiles) for i in range(tiles)])
                    for away, part in enumerate(parts[1:], 1)
                ]
        elif kind == "compress":
            index = owner_of[number]
            place = number - firsts[index]
            with jax.named_scope("compress"):
                ready[index], ahead[number] = compress(
                    [own_parts[number]] + others[number],
                    ahead.get(number - 1), taps, at, lens, limits, pulses, owners, number < len(chunks) - 1,
                    ready.get(index), len(groups[index]) - 1 - place, len(groups[index]),
                )
        elif kind == "send":
            with jax.named_scope("to_owners"):
                got[number] = lax.all_to_all(ready[number], "beam", split_axis=0, concat_axis=0)
        elif kind == "doppler":
            with jax.named_scope("doppler"):
                out = doppler(got[number], table, out, groups[number][-1][0], pulses)
        elif kind == "beams<beams":
            power, own_parts[number] = lax.optimization_barrier((power, own_parts[number]))
        elif kind == "beams<compress":
            own_parts[number[1]], own_parts[number[0]] = lax.optimization_barrier(
                (own_parts[number[1]], own_parts[number[0]])
            )
        elif kind == "arrived<beams":
            power, others[number][0] = lax.optimization_barrier((power, others[number][0]))
        elif kind == "arrived<doppler":
            table, others[number][0] = lax.optimization_barrier((table, others[number][0]))
        elif kind == "compress<beams":
            index = owner_of[number]
            power, ready[index] = lax.optimization_barrier((power, ready[index]))
        elif kind == "compress<doppler":
            table, ahead[number] = lax.optimization_barrier((table, ahead[number]))
        elif kind == "doppler<compress":
            ahead[number], out = lax.optimization_barrier((ahead[number], out))
        elif kind == "last<doppler":
            out, ready[number] = lax.optimization_barrier((out, ready[number]))
    return out


def solution(mesh):
    placed = (P(None, "tile", "beam"), P(None, None, "tile"), P(), P(), P(), P())
    return jax.shard_map(
        on_device,
        mesh=mesh,
        in_specs=placed,
        out_specs=P(("tile", "beam"), None, None, None),
        check_vma=False,
    )
```

```python
import functools
import math

import jax
import jax.numpy as jnp
import numpy as np
from jax import lax
from jax.experimental import pallas as pl
from jax.experimental.pallas import tpu as pltpu
from jax.sharding import PartitionSpec as P

G = 32
EPS = 1e-05
CHUNK = 8
TOGETHER = (2, 2)
STREAMED = (0, 1, 3)
NT = (((1,), (1,)), ((), ()))
TN = (((0,), (0,)), ((), ()))
MIB = 1024 * 1024


def params(mib):
    return pltpu.CompilerParams(vmem_limit_bytes=mib * MIB)


def busy(micros):
    return pl.CostEstimate(flops=int(micros * 1.15e9), bytes_accessed=1, transcendentals=0)


def block_of(size, most):
    return max(n for n in range(1, min(size, most) + 1) if size % n == 0)


def groups_of(gates):
    if CHUNK * sum(TOGETHER) != gates:
        return [[(0, gates)]]
    found, end = [], gates
    for count in TOGETHER:
        found.append([(end - CHUNK * (i + 1), CHUNK) for i in range(count)])
        end -= CHUNK * count
    return found


def in_hbm(*values):
    return [pltpu.with_memory_space_constraint(x, pltpu.HBM) for x in values]


def lookup_kernel(order_ref, lens_ref, limits_ref, near_ref, len_ref, limit_ref):
    tiles, mine = lax.axis_size("tile"), lax.axis_index("tile")
    beam_total, slots = order_ref.shape[1], len_ref.shape[1]
    for away in range(tiles):
        start = pl.multiple_of(lax.rem(mine + away, tiles) * slots, slots)
        near_ref[:, away * slots : (away + 1) * slots] = order_ref[:, pl.ds(start, slots)]
    wide = block_of(beam_total, 512)
    found = jnp.zeros((8, slots), jnp.float32)
    for first in range(0, beam_total, wide):
        at = slice(first, first + wide)
        lens, limits = lens_ref[:, at], limits_ref[:, at]
        row = lax.broadcasted_iota(jnp.int32, (8, wide), 0)
        values = jnp.where(row == 0, lens, jnp.where(row == 1, limits >> 5, limits & 31))
        beam = first + lax.broadcasted_iota(jnp.int32, (wide, slots), 0)
        pick = jnp.where(beam == near_ref[:, :slots], 1.0, 0.0).astype(jnp.bfloat16)
        found += jnp.dot(
            values.astype(jnp.float32).astype(jnp.bfloat16), pick, preferred_element_type=jnp.float32
        )
    found = found.astype(jnp.int32)
    len_ref[...] = found[0:1]
    limit_ref[...] = found[1:2] * 32 + found[2:3]


def lookup(order, code_len, dwell, slots):
    whole = pl.BlockSpec(memory_space=pltpu.VMEM)
    return pl.pallas_call(
        lookup_kernel,
        in_specs=[whole] * 3,
        out_specs=[whole] * 3,
        out_shape=[jax.ShapeDtypeStruct((1, size), jnp.int32) for size in (order.shape[0], slots, slots)],
        compiler_params=params(8),
        cost_estimate=busy(20),
        name="lookup",
    )(order[None, :], code_len[None, :], dwell[None, :])


def add_kernel(*refs):
    total = refs[0][...]
    for ref in refs[1:-1]:
        total = total + ref[...]
    refs[-1][...] = total


def add(*values):
    whole = pl.BlockSpec(memory_space=pltpu.VMEM)
    return pl.pallas_call(
        add_kernel,
        in_specs=[whole] * len(values),
        out_specs=whole,
        out_shape=jax.ShapeDtypeStruct(values[0].shape, values[0].dtype),
        compiler_params=params(1),
        cost_estimate=busy(1),
        name="add",
    )(*values)


def beam_kernel(samples, gates, gate, count, streamed, tiles, picks, echoes_ref, power_ref, order_ref, steer_ref, *rest):
    if streamed:
        steer_hbm, steer_ref, sem = steer_ref, rest[-2], rest[-1]
        rest = rest[:-2]
    out_refs, (scaled_ref, row_ref, picked_ref) = rest[:-3], rest[-3:]
    if len(picks) < tiles:
        *out_refs, beams_ref = out_refs
    _, chans, columns = echoes_ref.shape
    beam_total, wide = steer_ref.shape[1], row_ref.shape[0]
    steps = beam_total // wide

    def copy(part, step):
        at = pl.ds(step * wide, wide)
        return pltpu.make_async_copy(steer_hbm.at[part, at], steer_ref.at[part, at], sem.at[part, step])

    if streamed:
        for step in range(min(2, steps)):
            for part in range(2):
                copy(part, step).start()
    pulses = columns // gates
    rows = count * pulses
    row = lax.broadcasted_iota(jnp.int32, (rows, columns), 0)
    col = lax.broadcasted_iota(jnp.int32, (rows, columns), 1)
    source = (row % pulses) * gates + row // pulses + gate
    moved = jnp.where(source == col, 1.0, 0.0).astype(jnp.bfloat16)
    row_ref[...] = lax.broadcasted_iota(jnp.int32, row_ref.shape, 0)
    gain = lax.rsqrt(power_ref[...] / samples + EPS)
    real = lax.dot_general(moved, echoes_ref[0], NT, preferred_element_type=jnp.float32) * gain
    imag = lax.dot_general(moved, echoes_ref[1], NT, preferred_element_type=jnp.float32) * gain
    scaled_ref[:rows, :chans] = real.astype(jnp.bfloat16)
    scaled_ref[:rows, chans:] = (-imag).astype(jnp.bfloat16)
    scaled_ref[rows:, :chans] = imag.astype(jnp.bfloat16)
    scaled_ref[rows:, chans:] = real.astype(jnp.bfloat16)

    slots, tile_beams = row_ref.shape[1], beam_total // tiles
    starts = [start for tile in picks for start in range(tile * tile_beams, (tile + 1) * tile_beams, slots)]
    for step in range(steps):
        at = slice(step * wide, (step + 1) * wide)
        if streamed:
            for part in range(2):
                copy(part, step).wait()
                if step + 2 < steps:
                    copy(part, step + 2).start()
        beams = lax.dot_general(scaled_ref[:, :chans], steer_ref[0, at], NT, preferred_element_type=jnp.float32)
        beams += lax.dot_general(scaled_ref[:, chans:], steer_ref[1, at], NT, preferred_element_type=jnp.float32)
        beams = beams.astype(jnp.bfloat16)
        if len(picks) < tiles:
            beams_ref[:, at] = beams
        for start in starts:
            wanted = order_ref[:, start : start + slots] - step * wide
            pick = jnp.where(row_ref[...] == wanted, 1.0, 0.0).astype(jnp.bfloat16)
            picked = jnp.dot(beams, pick, preferred_element_type=jnp.float32)
            if step > 0:
                picked += picked_ref[:, start : start + slots]
            picked_ref[:, start : start + slots] = picked

    for tile, out_ref in zip(picks, out_refs):
        out_ref[...] = picked_ref[:, tile * tile_beams : (tile + 1) * tile_beams].astype(jnp.bfloat16)


def own_kernel(beams_ref, order_ref, out_ref, row_ref):
    beam_total, slots = beams_ref.shape[1], out_ref.shape[1]
    wide, some = row_ref.shape
    row_ref[...] = lax.broadcasted_iota(jnp.int32, row_ref.shape, 0)
    for start in range(0, slots, some):
        picked = None
        for first in range(0, beam_total, wide):
            wanted = order_ref[:, start : start + some] - first
            pick = jnp.where(row_ref[...] == wanted, 1.0, 0.0).astype(jnp.bfloat16)
            term = jnp.dot(beams_ref[:, first : first + wide], pick, preferred_element_type=jnp.float32)
            picked = term if picked is None else picked + term
        out_ref[:, start : start + some] = picked.astype(jnp.bfloat16)


def pick_own(beams, order, tiles):
    rows, beam_total = beams.shape
    slots = beam_total // tiles
    whole = pl.BlockSpec(memory_space=pltpu.VMEM)
    return pl.pallas_call(
        own_kernel,
        in_specs=[whole] * 2,
        out_specs=whole,
        out_shape=pltpu.VMEM((rows, slots), jnp.bfloat16),
        scratch_shapes=[pltpu.VMEM((block_of(beam_total, 512), block_of(slots, 512)), jnp.int32)],
        compiler_params=params(16),
        cost_estimate=busy(2),
        name="own",
    )(pltpu.with_memory_space_constraint(beams, pltpu.VMEM), order)


def form_beams(echoes, power, order, steer, gates, gate, count, samples, tiles, streamed, picks):
    _, chans, columns = echoes.shape
    beam_total = steer.shape[1]
    tile_beams = beam_total // tiles
    rows = columns // gates * count
    wide = block_of(beam_total, 512)
    echoes = pltpu.with_memory_space_constraint(echoes, pltpu.VMEM)
    steer = pltpu.with_memory_space_constraint(steer, pltpu.HBM if streamed else pltpu.VMEM)
    whole = pl.BlockSpec(memory_space=pltpu.VMEM)
    spaces = [pltpu.HBM if tile else pltpu.VMEM for tile in picks]
    out_shape = [space((2 * rows, tile_beams), jnp.bfloat16) for space in spaces]
    if len(picks) < tiles:
        out_shape.append(pltpu.VMEM((2 * rows, beam_total), jnp.bfloat16))
    return pl.pallas_call(
        functools.partial(beam_kernel, samples, gates, gate, count, streamed, tiles, picks),
        in_specs=[whole] * 3 + [pl.BlockSpec(memory_space=pl.ANY) if streamed else whole],
        out_specs=[whole] * len(out_shape),
        out_shape=out_shape,
        scratch_shapes=[
            pltpu.VMEM((2 * rows, 2 * chans), jnp.bfloat16),
            pltpu.VMEM((wide, block_of(tile_beams, 512)), jnp.int32),
            pltpu.VMEM((2 * rows, beam_total), jnp.float32),
        ]
        + ([pltpu.VMEM(steer.shape, steer.dtype), pltpu.SemaphoreType.DMA((2, beam_total // wide))] if streamed else []),
        compiler_params=params(24),
        cost_estimate=busy(9),
        name="beams",
    )(echoes, power, order, steer)


def compress_kernel(pulses, taps, parts_in, halo, shared, keep_ahead, place, code_ref, at_ref, lens_ref, limits_ref, *rest):
    part_refs, rest = rest[:parts_in], rest[parts_in:]
    if halo:
        ahead_ref, rest = rest[0], rest[1:]
    out_hbm, rest = rest[shared], rest[shared + 1 :]
    away = keep_ahead and place == 0
    if away:
        beams_hbm, beams_ref, beams_sem, rest = rest[0], rest[-2], rest[-1], rest[1:-2]
    elif keep_ahead:
        beams_ref, rest = rest[0], rest[1:]
    wide_ref, laid_ref, sem = rest
    rows, tile_beams = part_refs[0].shape[0] // 2, part_refs[0].shape[1]
    edge = (taps - 1) * pulses
    lanes = wide_ref.shape[2]
    own = laid_ref.shape[2] // 2
    some = lanes // own

    def copy(block):
        at = pl.ds(block * some, some)
        return pltpu.make_async_copy(
            laid_ref.at[at], out_hbm.at[at, pl.ds(place * rows, rows)], sem.at[block]
        )

    def beams_copy(block):
        at = pl.ds(block * lanes, lanes)
        return pltpu.make_async_copy(beams_ref.at[:, :, at], beams_hbm.at[:, :, at], beams_sem.at[block])

    for block in range(tile_beams // lanes):
        at = slice(block * lanes, (block + 1) * lanes)
        for part in range(2):
            total = part_refs[0][part * rows : (part + 1) * rows, at].astype(jnp.float32)
            for ref in part_refs[1:]:
                total += ref[part * rows : (part + 1) * rows, at].astype(jnp.float32)
            rounded = total.astype(jnp.bfloat16)
            if keep_ahead:
                beams_ref[part, :, at] = rounded[:edge]
            wide_ref[part, :rows] = rounded.astype(jnp.float32)
            if halo:
                wide_ref[part, rows:] = ahead_ref[part, :, at].astype(jnp.float32)
            else:
                wide_ref[part, rows:] = jnp.zeros((edge, lanes), jnp.float32)
        if away:
            beams_copy(block).start()
        lens, limits = lens_ref[:, at], limits_ref[:, at]
        pulse = at_ref[0] + lax.broadcasted_iota(jnp.int32, (pulses, lanes), 0)
        keep = pulse < limits
        factors = [
            tuple(
                jnp.where(tap < lens, code_ref[part : part + 1, tap : tap + 1].astype(jnp.float32), 0.0)
                for part in range(2)
            )
            for tap in range(taps)
        ]
        for gate in range(rows // pulses):
            real = imag = None
            for tap, (code_re, code_im) in enumerate(factors):
                start = (gate + tap) * pulses
                shift_re = wide_ref[0, start : start + pulses]
                shift_im = wide_ref[1, start : start + pulses]
                term_re = code_re * shift_re + code_im * shift_im
                term_im = code_re * shift_im - code_im * shift_re
                real = term_re if real is None else real + term_re
                imag = term_im if imag is None else imag + term_im
            real = jnp.where(keep, real, 0.0)
            imag = jnp.where(keep, imag, 0.0)
            for owner in range(some):
                line = slice(owner * own, (owner + 1) * own)
                joined = jnp.concatenate([real[:, line], imag[:, line]], axis=1).astype(jnp.bfloat16)
                laid_ref[block * some + owner, gate * pulses : (gate + 1) * pulses] = joined
        copy(block).start()
    for block in range(tile_beams // lanes):
        copy(block).wait()
        if away:
            beams_copy(block).wait()


def compress(parts, ahead, code, at, lens, limits, pulses, owners, keep_ahead, ready, place, places):
    taps = code.shape[1]
    rows, tile_beams = parts[0].shape[0] // 2, parts[0].shape[1]
    own = tile_beams // owners
    lanes = block_of(tile_beams, 256)
    edge = (taps - 1) * pulses
    whole, apart = pl.BlockSpec(memory_space=pltpu.VMEM), pl.BlockSpec(memory_space=pl.ANY)
    scalars = pl.BlockSpec(memory_space=pltpu.SMEM)
    out_shape = [pltpu.HBM((owners, places * rows, 2 * own), jnp.bfloat16)]
    if keep_ahead:
        out_shape.append((pltpu.VMEM if place else pltpu.HBM)((2, edge, tile_beams), jnp.bfloat16))
    near = [pltpu.with_memory_space_constraint(x, pltpu.VMEM) for x in parts + ([] if ahead is None else [ahead])]
    shared = [] if ready is None else in_hbm(ready)
    done = pl.pallas_call(
        functools.partial(
            compress_kernel, pulses, taps, len(parts), ahead is not None, len(shared), keep_ahead, place
        ),
        in_specs=[whole, scalars, whole, whole] + [whole] * len(near) + [apart] * len(shared),
        out_specs=[apart] + [whole if place else apart] * keep_ahead,
        out_shape=out_shape,
        scratch_shapes=[
            pltpu.VMEM((2, rows + edge, lanes), jnp.float32),
            pltpu.VMEM((owners, rows, 2 * own), jnp.bfloat16),
            pltpu.SemaphoreType.DMA((tile_beams // lanes,)),
        ]
        + (
            [pltpu.VMEM((2, edge, tile_beams), jnp.bfloat16), pltpu.SemaphoreType.DMA((tile_beams // lanes,))]
            if keep_ahead and place == 0
            else []
        ),
        input_output_aliases={4 + len(near): 0} if shared else {},
        compiler_params=params(16),
        cost_estimate=busy(3),
        name="compress",
    )(code, at, lens, limits, *near, *shared)
    return done if keep_ahead else (done[0], None)


def doppler_kernel(pulses, got_ref, table_ref, *rest):
    out_ref, lines_ref = rest[-2:]
    owners, rows, lanes = got_ref.shape
    own, bins = lanes // 2, table_ref.shape[1] // 2
    gates = rows // pulses
    some = block_of(gates, max(1, 512 // lanes))
    for first in range(0, gates, some):
        values = jnp.concatenate(
            [
                got_ref[:, gate * pulses : (gate + 1) * pulses].reshape(owners * pulses, lanes)
                for gate in range(first, first + some)
            ],
            axis=1,
        )
        both = lax.dot_general(values, table_ref[...], TN, preferred_element_type=jnp.float32)
        for index in range(some):
            gate, start = first + index, index * lanes
            upper, lower = both[start : start + own], both[start + own : start + lanes]
            real = upper[:, :bins] - lower[:, bins:]
            imag = lower[:, :bins] + upper[:, bins:]
            for part, line in enumerate((real, imag)):
                for at in range(lines_ref.shape[0]):
                    lines_ref[at, pl.ds(part * gates + gate, own, stride=2 * gates), :] = line[
                        :, at * 128 : (at + 1) * 128
                    ]
    for at in range(lines_ref.shape[0]):
        out_ref[:, :, :, at * 128 : (at + 1) * 128] = lines_ref[at].reshape(own, 2, gates, 128)


def doppler(got, table, out, first, pulses):
    owners, rows, lanes = got.shape
    own, bins, gates = lanes // 2, table.shape[1] // 2, rows // pulses
    some = CHUNK if gates % CHUNK == 0 else gates
    return pl.pallas_call(
        functools.partial(doppler_kernel, pulses),
        grid=(gates // some,),
        in_specs=[
            pl.BlockSpec((owners, some * pulses, lanes), lambda i: (0, i, 0)),
            pl.BlockSpec(table.shape, lambda i: (0, 0)),
        ]
        + ([] if out is None else [pl.BlockSpec(memory_space=pl.ANY)]),
        out_specs=pl.BlockSpec((own, 2, some, bins), lambda i: (0, 0, first // some + i, 0)),
        out_shape=jax.ShapeDtypeStruct((own, 2, G, bins), jnp.float32),
        scratch_shapes=[pltpu.VMEM((bins // 128, own * 2 * some, 128), jnp.float32)],
        input_output_aliases={} if out is None else {2: 0},
        compiler_params=params(24),
        cost_estimate=busy(3),
        name="doppler",
    )(got, table, *([] if out is None else [out]))


def phase_table(total):
    angle = np.outer(np.arange(total), np.arange(total)) % total * (2.0 * math.pi / total)
    return np.concatenate([np.cos(angle), -np.sin(angle)], axis=1) / math.sqrt(total)


def sum_over(values, axis):
    size = lax.axis_size(axis)
    if size & (size - 1):
        return lax.psum(values, axis)
    step = 1
    while step < size:
        steps = [step * i for i in (1, 2, 3) if step * i < size] if step * 2 < size else [step]
        values = add(
            values, *(lax.ppermute(values, axis, [(i, i ^ away) for i in range(size)]) for away in steps)
        )
        step *= len(steps) + 1
    return values


def order_of(groups):
    count = sum(len(group) for group in groups)
    if count == 1:
        return [("beams", 0), ("exchange", 0), ("own", 0), ("compress", 0), ("send", 0), ("doppler", 0)]
    return [
        ("beams", 0),
        ("exchange", 0),
        ("beams<beams", 0),
        ("beams", 1),
        ("exchange", 1),
        ("beams<compress", (1, 0)),
        ("own", 0),
        ("beams<beams", 1),
        ("beams", 2),
        ("exchange", 2),
        ("beams<compress", (2, 0)),
        ("compress", 0),
        ("compress", 1),
        ("compress<beams", 1),
        ("send", 0),
        ("beams", 3),
        ("exchange", 3),
        ("beams<compress", (3, 2)),
        ("compress", 2),
        ("compress", 3),
        ("send", 1),
        ("doppler", 0),
        ("doppler", 1),
    ]


def on_device(echoes, steer, code, beam_order, dwell, code_len):
    tiles, owners = lax.axis_size("tile"), lax.axis_size("beam")
    columns = echoes.shape[2]
    beam_total = steer.shape[1]
    pulses = columns // G
    total = pulses * owners
    tile_beams = beam_total // tiles
    own = tile_beams // owners

    values = echoes.astype(jnp.float32)
    power = sum_over(jnp.sum(values * values, axis=(0, 2))[None, :], "beam")

    order, lens, limits = lookup(beam_order, code_len, dwell, tile_beams)
    at = (lax.axis_index("beam") * pulses)[None]
    table = jnp.asarray(phase_table(total).astype(jnp.bfloat16))

    groups = groups_of(G)
    chunks = [chunk for group in groups for chunk in group]
    owner_of = [index for index, group in enumerate(groups) for _ in group]
    firsts = [owner_of.index(index) for index in range(len(groups))]
    own_parts, others, ready, ahead, got, out = {}, {}, {}, {}, {}, None
    for kind, number in order_of(groups):
        if kind == "beams":
            gate, gates = chunks[number]
            with jax.named_scope("beams"):
                picks = tuple(range(1 if number == 0 and tiles > 1 else 0, tiles))
                parts = form_beams(
                    echoes, power, order, steer, G, gate, gates, total * G, tiles, number in STREAMED, picks
                )
            if len(picks) < tiles:
                parts = [parts[-1], *parts[:-1]]
            own_parts[number], *others[number] = parts
        elif kind == "own":
            if tiles > 1:
                with jax.named_scope("beams"):
                    own_parts[number] = pick_own(own_parts[number], order, tiles)
        elif kind == "exchange":
            with jax.named_scope("tile_sum"):
                others[number] = [
                    lax.ppermute(part, "tile", [(i, (i + away) % tiles) for i in range(tiles)])
                    for away, part in enumerate(others[number], 1)
                ]
        elif kind == "arrived<exchange":
            others[number[0]][0], others[number[1]][0] = lax.optimization_barrier(
                (others[number[0]][0], others[number[1]][0])
            )
        elif kind == "compress":
            index = owner_of[number]
            place = number - firsts[index]
            with jax.named_scope("compress"):
                ready[index], ahead[number] = compress(
                    [own_parts[number]] + others[number],
                    ahead.get(number - 1), code, at, lens, limits, pulses, owners, number < len(chunks) - 1,
                    ready.get(index), len(groups[index]) - 1 - place, len(groups[index]),
                )
        elif kind == "send":
            with jax.named_scope("to_owners"):
                got[number] = lax.all_to_all(ready[number], "beam", split_axis=0, concat_axis=0)
        elif kind == "doppler":
            with jax.named_scope("doppler"):
                out = doppler(got[number], table, out, groups[number][-1][0], pulses)
        elif kind == "beams<beams":
            power, own_parts[number] = lax.optimization_barrier((power, own_parts[number]))
        elif kind == "beams<compress":
            own_parts[number[1]], own_parts[number[0]] = lax.optimization_barrier(
                (own_parts[number[1]], own_parts[number[0]])
            )
        elif kind == "arrived<beams":
            power, others[number][0] = lax.optimization_barrier((power, others[number][0]))
        elif kind == "arrived<doppler":
            table, others[number][0] = lax.optimization_barrier((table, others[number][0]))
        elif kind == "compress<exchange":
            index = owner_of[number[0]]
            others[number[1]][0], ready[index] = lax.optimization_barrier((others[number[1]][0], ready[index]))
        elif kind == "compress<beams":
            index = owner_of[number]
            power, ready[index] = lax.optimization_barrier((power, ready[index]))
        elif kind == "compress<doppler":
            table, ahead[number] = lax.optimization_barrier((table, ahead[number]))
        elif kind == "doppler<compress":
            ahead[number], out = lax.optimization_barrier((ahead[number], out))
        elif kind == "last<doppler":
            out, ready[number] = lax.optimization_barrier((out, ready[number]))
    return out


def solution(mesh):
    placed = (P(None, "tile", "beam"), P(None, None, "tile"), P(), P(), P(), P())
    return jax.shard_map(
        on_device,
        mesh=mesh,
        in_specs=placed,
        out_specs=P(("tile", "beam"), None, None, None),
        check_vma=False,
    )
```

```python
import functools
import math

import jax
import jax.numpy as jnp
import numpy as np
from jax import lax
from jax.experimental import pallas as pl
from jax.experimental.pallas import tpu as pltpu
from jax.sharding import PartitionSpec as P

G = 32
EPS = 1e-05
CHUNK = 8
TOGETHER = (2, 2)
STREAMED = (0, 1, 3)
LATER = (0, 3)
NT = (((1,), (1,)), ((), ()))
TN = (((0,), (0,)), ((), ()))
MIB = 1024 * 1024


def params(mib):
    return pltpu.CompilerParams(vmem_limit_bytes=mib * MIB)


def busy(micros):
    return pl.CostEstimate(flops=int(micros * 1.15e9), bytes_accessed=1, transcendentals=0)


def block_of(size, most):
    return max(n for n in range(1, min(size, most) + 1) if size % n == 0)


def groups_of(gates):
    if CHUNK * sum(TOGETHER) != gates:
        return [[(0, gates)]]
    found, end = [], gates
    for count in TOGETHER:
        found.append([(end - CHUNK * (i + 1), CHUNK) for i in range(count)])
        end -= CHUNK * count
    return found


def in_hbm(*values):
    return [pltpu.with_memory_space_constraint(x, pltpu.HBM) for x in values]


def lookup_kernel(order_ref, lens_ref, limits_ref, near_ref, len_ref, limit_ref):
    tiles, mine = lax.axis_size("tile"), lax.axis_index("tile")
    beam_total, slots = order_ref.shape[1], len_ref.shape[1]
    for away in range(tiles):
        start = pl.multiple_of(lax.rem(mine + away, tiles) * slots, slots)
        near_ref[:, away * slots : (away + 1) * slots] = order_ref[:, pl.ds(start, slots)]
    wide = block_of(beam_total, 512)
    found = jnp.zeros((8, slots), jnp.float32)
    for first in range(0, beam_total, wide):
        at = slice(first, first + wide)
        lens, limits = lens_ref[:, at], limits_ref[:, at]
        row = lax.broadcasted_iota(jnp.int32, (8, wide), 0)
        values = jnp.where(row == 0, lens, jnp.where(row == 1, limits >> 5, limits & 31))
        beam = first + lax.broadcasted_iota(jnp.int32, (wide, slots), 0)
        pick = jnp.where(beam == near_ref[:, :slots], 1.0, 0.0).astype(jnp.bfloat16)
        found += jnp.dot(
            values.astype(jnp.float32).astype(jnp.bfloat16), pick, preferred_element_type=jnp.float32
        )
    found = found.astype(jnp.int32)
    len_ref[...] = found[0:1]
    limit_ref[...] = found[1:2] * 32 + found[2:3]


def lookup(order, code_len, dwell, slots):
    whole = pl.BlockSpec(memory_space=pltpu.VMEM)
    return pl.pallas_call(
        lookup_kernel,
        in_specs=[whole] * 3,
        out_specs=[whole] * 3,
        out_shape=[jax.ShapeDtypeStruct((1, size), jnp.int32) for size in (order.shape[0], slots, slots)],
        compiler_params=params(8),
        cost_estimate=busy(20),
        name="lookup",
    )(order[None, :], code_len[None, :], dwell[None, :])


def add_kernel(*refs):
    total = refs[0][...]
    for ref in refs[1:-1]:
        total = total + ref[...]
    refs[-1][...] = total


def add(*values):
    whole = pl.BlockSpec(memory_space=pltpu.VMEM)
    return pl.pallas_call(
        add_kernel,
        in_specs=[whole] * len(values),
        out_specs=whole,
        out_shape=jax.ShapeDtypeStruct(values[0].shape, values[0].dtype),
        compiler_params=params(1),
        cost_estimate=busy(1),
        name="add",
    )(*values)


def beam_kernel(samples, gates, gate, count, streamed, tiles, picks, echoes_ref, power_ref, order_ref, steer_ref, *rest):
    if streamed:
        steer_hbm, steer_ref, sem = steer_ref, rest[-2], rest[-1]
        rest = rest[:-2]
    out_refs, (scaled_ref, row_ref, picked_ref) = rest[:-3], rest[-3:]
    if len(picks) < tiles:
        *out_refs, beams_ref = out_refs
    _, chans, columns = echoes_ref.shape
    beam_total, wide = steer_ref.shape[1], row_ref.shape[0]
    steps = beam_total // wide

    def copy(part, step):
        at = pl.ds(step * wide, wide)
        return pltpu.make_async_copy(steer_hbm.at[part, at], steer_ref.at[part, at], sem.at[part, step])

    if streamed:
        for part in range(2):
            copy(part, 0).start()
    pulses = columns // gates
    rows = count * pulses
    row = lax.broadcasted_iota(jnp.int32, (rows, columns), 0)
    col = lax.broadcasted_iota(jnp.int32, (rows, columns), 1)
    source = (row % pulses) * gates + row // pulses + gate
    moved = jnp.where(source == col, 1.0, 0.0).astype(jnp.bfloat16)
    row_ref[...] = lax.broadcasted_iota(jnp.int32, row_ref.shape, 0)
    gain = lax.rsqrt(power_ref[...] / samples + EPS)
    real = lax.dot_general(moved, echoes_ref[0], NT, preferred_element_type=jnp.float32) * gain
    imag = lax.dot_general(moved, echoes_ref[1], NT, preferred_element_type=jnp.float32) * gain
    scaled_ref[:rows, :chans] = real.astype(jnp.bfloat16)
    scaled_ref[:rows, chans:] = (-imag).astype(jnp.bfloat16)
    scaled_ref[rows:, :chans] = imag.astype(jnp.bfloat16)
    scaled_ref[rows:, chans:] = real.astype(jnp.bfloat16)

    if streamed and steps > 1:
        for part in range(2):
            copy(part, 1).start()
    slots, tile_beams = row_ref.shape[1], beam_total // tiles
    starts = [start for tile in picks for start in range(tile * tile_beams, (tile + 1) * tile_beams, slots)]
    for step in range(steps):
        at = slice(step * wide, (step + 1) * wide)
        if streamed:
            for part in range(2):
                copy(part, step).wait()
                if step + 2 < steps:
                    copy(part, step + 2).start()
        beams = lax.dot_general(scaled_ref[:, :chans], steer_ref[0, at], NT, preferred_element_type=jnp.float32)
        beams += lax.dot_general(scaled_ref[:, chans:], steer_ref[1, at], NT, preferred_element_type=jnp.float32)
        beams = beams.astype(jnp.bfloat16)
        if len(picks) < tiles:
            beams_ref[:, at] = beams
        for start in starts:
            wanted = order_ref[:, start : start + slots] - step * wide
            pick = jnp.where(row_ref[...] == wanted, 1.0, 0.0).astype(jnp.bfloat16)
            picked = jnp.dot(beams, pick, preferred_element_type=jnp.float32)
            if step > 0:
                picked += picked_ref[:, start : start + slots]
            picked_ref[:, start : start + slots] = picked

    for tile, out_ref in zip(picks, out_refs):
        out_ref[...] = picked_ref[:, tile * tile_beams : (tile + 1) * tile_beams].astype(jnp.bfloat16)


def own_kernel(beams_ref, order_ref, out_ref, row_ref):
    beam_total, slots = beams_ref.shape[1], out_ref.shape[1]
    wide, some = row_ref.shape
    row_ref[...] = lax.broadcasted_iota(jnp.int32, row_ref.shape, 0)
    for start in range(0, slots, some):
        picked = None
        for first in range(0, beam_total, wide):
            wanted = order_ref[:, start : start + some] - first
            pick = jnp.where(row_ref[...] == wanted, 1.0, 0.0).astype(jnp.bfloat16)
            term = jnp.dot(beams_ref[:, first : first + wide], pick, preferred_element_type=jnp.float32)
            picked = term if picked is None else picked + term
        out_ref[:, start : start + some] = picked.astype(jnp.bfloat16)


def pick_own(beams, order, tiles):
    rows, beam_total = beams.shape
    slots = beam_total // tiles
    whole = pl.BlockSpec(memory_space=pltpu.VMEM)
    return pl.pallas_call(
        own_kernel,
        in_specs=[whole] * 2,
        out_specs=whole,
        out_shape=pltpu.VMEM((rows, slots), jnp.bfloat16),
        scratch_shapes=[pltpu.VMEM((block_of(beam_total, 512), block_of(slots, 512)), jnp.int32)],
        compiler_params=params(16),
        cost_estimate=busy(2),
        name="own",
    )(pltpu.with_memory_space_constraint(beams, pltpu.VMEM), order)


def form_beams(echoes, power, order, steer, gates, gate, count, samples, tiles, streamed, picks, micros):
    _, chans, columns = echoes.shape
    beam_total = steer.shape[1]
    tile_beams = beam_total // tiles
    rows = columns // gates * count
    wide = block_of(beam_total, 512)
    echoes = pltpu.with_memory_space_constraint(echoes, pltpu.VMEM)
    steer = pltpu.with_memory_space_constraint(steer, pltpu.HBM if streamed else pltpu.VMEM)
    whole = pl.BlockSpec(memory_space=pltpu.VMEM)
    spaces = [pltpu.HBM if tile else pltpu.VMEM for tile in picks]
    out_shape = [space((2 * rows, tile_beams), jnp.bfloat16) for space in spaces]
    if len(picks) < tiles:
        out_shape.append(pltpu.VMEM((2 * rows, beam_total), jnp.bfloat16))
    return pl.pallas_call(
        functools.partial(beam_kernel, samples, gates, gate, count, streamed, tiles, picks),
        in_specs=[whole] * 3 + [pl.BlockSpec(memory_space=pl.ANY) if streamed else whole],
        out_specs=[whole] * len(out_shape),
        out_shape=out_shape,
        scratch_shapes=[
            pltpu.VMEM((2 * rows, 2 * chans), jnp.bfloat16),
            pltpu.VMEM((wide, block_of(tile_beams, 512)), jnp.int32),
            pltpu.VMEM((2 * rows, beam_total), jnp.float32),
        ]
        + ([pltpu.VMEM(steer.shape, steer.dtype), pltpu.SemaphoreType.DMA((2, beam_total // wide))] if streamed else []),
        compiler_params=params(24),
        cost_estimate=busy(micros),
        name="beams",
    )(echoes, power, order, steer)


def compress_kernel(pulses, taps, parts_in, halo, shared, keep_ahead, place, code_ref, at_ref, lens_ref, limits_ref, *rest):
    part_refs, rest = rest[:parts_in], rest[parts_in:]
    if halo:
        ahead_ref, rest = rest[0], rest[1:]
    out_hbm, rest = rest[shared], rest[shared + 1 :]
    away = keep_ahead and place == 0
    if away:
        beams_hbm, beams_ref, beams_sem, rest = rest[0], rest[-2], rest[-1], rest[1:-2]
    elif keep_ahead:
        beams_ref, rest = rest[0], rest[1:]
    wide_ref, laid_ref, sem = rest
    rows, tile_beams = part_refs[0].shape[0] // 2, part_refs[0].shape[1]
    edge = (taps - 1) * pulses
    lanes = wide_ref.shape[2]
    own = laid_ref.shape[2] // 2
    some = lanes // own

    def copy(block):
        at = pl.ds(block * some, some)
        return pltpu.make_async_copy(
            laid_ref.at[at], out_hbm.at[at, pl.ds(place * rows, rows)], sem.at[block]
        )

    def beams_copy(block):
        at = pl.ds(block * lanes, lanes)
        return pltpu.make_async_copy(beams_ref.at[:, :, at], beams_hbm.at[:, :, at], beams_sem.at[block])

    for block in range(tile_beams // lanes):
        at = slice(block * lanes, (block + 1) * lanes)
        for part in range(2):
            total = part_refs[0][part * rows : (part + 1) * rows, at].astype(jnp.float32)
            for ref in part_refs[1:]:
                total += ref[part * rows : (part + 1) * rows, at].astype(jnp.float32)
            rounded = total.astype(jnp.bfloat16)
            if keep_ahead:
                beams_ref[part, :, at] = rounded[:edge]
            wide_ref[part, :rows] = rounded.astype(jnp.float32)
            if halo:
                wide_ref[part, rows:] = ahead_ref[part, :, at].astype(jnp.float32)
            else:
                wide_ref[part, rows:] = jnp.zeros((edge, lanes), jnp.float32)
        if away:
            beams_copy(block).start()
        lens, limits = lens_ref[:, at], limits_ref[:, at]
        pulse = at_ref[0] + lax.broadcasted_iota(jnp.int32, (pulses, lanes), 0)
        keep = pulse < limits
        factors = [
            tuple(
                jnp.where(tap < lens, code_ref[part : part + 1, tap : tap + 1].astype(jnp.float32), 0.0)
                for part in range(2)
            )
            for tap in range(taps)
        ]
        for gate in range(rows // pulses):
            real = imag = None
            for tap, (code_re, code_im) in enumerate(factors):
                start = (gate + tap) * pulses
                shift_re = wide_ref[0, start : start + pulses]
                shift_im = wide_ref[1, start : start + pulses]
                term_re = code_re * shift_re + code_im * shift_im
                term_im = code_re * shift_im - code_im * shift_re
                real = term_re if real is None else real + term_re
                imag = term_im if imag is None else imag + term_im
            real = jnp.where(keep, real, 0.0)
            imag = jnp.where(keep, imag, 0.0)
            for owner in range(some):
                line = slice(owner * own, (owner + 1) * own)
                joined = jnp.concatenate([real[:, line], imag[:, line]], axis=1).astype(jnp.bfloat16)
                laid_ref[block * some + owner, gate * pulses : (gate + 1) * pulses] = joined
        copy(block).start()
    for block in range(tile_beams // lanes):
        copy(block).wait()
        if away:
            beams_copy(block).wait()


def compress(parts, ahead, code, at, lens, limits, pulses, owners, keep_ahead, ready, place, places, micros):
    taps = code.shape[1]
    rows, tile_beams = parts[0].shape[0] // 2, parts[0].shape[1]
    own = tile_beams // owners
    lanes = block_of(tile_beams, 256)
    edge = (taps - 1) * pulses
    whole, apart = pl.BlockSpec(memory_space=pltpu.VMEM), pl.BlockSpec(memory_space=pl.ANY)
    scalars = pl.BlockSpec(memory_space=pltpu.SMEM)
    out_shape = [pltpu.HBM((owners, places * rows, 2 * own), jnp.bfloat16)]
    if keep_ahead:
        out_shape.append((pltpu.VMEM if place else pltpu.HBM)((2, edge, tile_beams), jnp.bfloat16))
    near = [pltpu.with_memory_space_constraint(x, pltpu.VMEM) for x in parts + ([] if ahead is None else [ahead])]
    shared = [] if ready is None else in_hbm(ready)
    done = pl.pallas_call(
        functools.partial(
            compress_kernel, pulses, taps, len(parts), ahead is not None, len(shared), keep_ahead, place
        ),
        in_specs=[whole, scalars, whole, whole] + [whole] * len(near) + [apart] * len(shared),
        out_specs=[apart] + [whole if place else apart] * keep_ahead,
        out_shape=out_shape,
        scratch_shapes=[
            pltpu.VMEM((2, rows + edge, lanes), jnp.float32),
            pltpu.VMEM((owners, rows, 2 * own), jnp.bfloat16),
            pltpu.SemaphoreType.DMA((tile_beams // lanes,)),
        ]
        + (
            [pltpu.VMEM((2, edge, tile_beams), jnp.bfloat16), pltpu.SemaphoreType.DMA((tile_beams // lanes,))]
            if keep_ahead and place == 0
            else []
        ),
        input_output_aliases={4 + len(near): 0} if shared else {},
        compiler_params=params(16),
        cost_estimate=busy(micros),
        name="compress",
    )(code, at, lens, limits, *near, *shared)
    return done if keep_ahead else (done[0], None)


def doppler_kernel(pulses, first, some, got_ref, table_ref, *rest):
    out_hbm, lines_ref, block_ref, sem = rest[-4:]
    owners, rows, lanes = got_ref.shape
    own, bins = lanes // 2, table_ref.shape[1] // 2
    gates = rows // pulses
    batch = block_of(some, max(1, 512 // lanes))

    def copy(block):
        at = pl.ds(first + block * some, some)
        return pltpu.make_async_copy(block_ref.at[block], out_hbm.at[:, :, at], sem.at[block])

    for block in range(gates // some):
        for start in range(0, some, batch):
            values = jnp.concatenate(
                [
                    got_ref[:, gate * pulses : (gate + 1) * pulses].reshape(owners * pulses, lanes)
                    for gate in range(block * some + start, block * some + start + batch)
                ],
                axis=1,
            )
            both = lax.dot_general(values, table_ref[...], TN, preferred_element_type=jnp.float32)
            for index in range(batch):
                upper = both[index * lanes : index * lanes + own]
                lower = both[index * lanes + own : (index + 1) * lanes]
                real = upper[:, :bins] - lower[:, bins:]
                imag = lower[:, :bins] + upper[:, bins:]
                for part, line in enumerate((real, imag)):
                    for at in range(lines_ref.shape[0]):
                        to = pl.ds(part * some + start + index, own, stride=2 * some)
                        lines_ref[at, to, :] = line[:, at * 128 : (at + 1) * 128]
        for at in range(lines_ref.shape[0]):
            block_ref[block, :, :, :, at * 128 : (at + 1) * 128] = lines_ref[at].reshape(own, 2, some, 128)
        copy(block).start()
    for block in range(gates // some):
        copy(block).wait()


def doppler(got, table, out, first, pulses):
    owners, rows, lanes = got.shape
    own, bins, gates = lanes // 2, table.shape[1] // 2, rows // pulses
    some = CHUNK if gates % CHUNK == 0 else gates
    whole, apart = pl.BlockSpec(memory_space=pltpu.VMEM), pl.BlockSpec(memory_space=pl.ANY)
    before = [] if out is None else [out]
    return pl.pallas_call(
        functools.partial(doppler_kernel, pulses, first, some),
        in_specs=[whole, whole] + [apart] * len(before),
        out_specs=apart,
        out_shape=jax.ShapeDtypeStruct((own, 2, G, bins), jnp.float32),
        scratch_shapes=[
            pltpu.VMEM((bins // 128, own * 2 * some, 128), jnp.float32),
            pltpu.VMEM((gates // some, own, 2, some, bins), jnp.float32),
            pltpu.SemaphoreType.DMA((gates // some,)),
        ],
        input_output_aliases={2: 0} if before else {},
        compiler_params=params(24),
        cost_estimate=busy(3),
        name="doppler",
    )(pltpu.with_memory_space_constraint(got, pltpu.VMEM), table, *before)


def phase_table(total):
    angle = np.outer(np.arange(total), np.arange(total)) % total * (2.0 * math.pi / total)
    return np.concatenate([np.cos(angle), -np.sin(angle)], axis=1) / math.sqrt(total)


def sum_over(values, axis):
    size = lax.axis_size(axis)
    if size & (size - 1):
        return lax.psum(values, axis)
    step = 1
    while step < size:
        steps = [step * i for i in (1, 2, 3) if step * i < size] if step * 2 < size else [step]
        values = add(
            values, *(lax.ppermute(values, axis, [(i, i ^ away) for i in range(size)]) for away in steps)
        )
        step *= len(steps) + 1
    return values


def order_of(groups):
    count = sum(len(group) for group in groups)
    if count == 1:
        return [("beams", 0), ("exchange", 0), ("own", 0), ("compress", 0), ("send", 0), ("doppler", 0)]
    return [
        ("beams", 0),
        ("exchange", 0),
        ("beams<beams", 0),
        ("beams", 1),
        ("exchange", 1),
        ("beams<compress", (1, 0)),
        ("own", 0),
        ("beams<beams", 1),
        ("beams", 2),
        ("beams<compress", (2, 0)),
        ("compress", 0),
        ("compress<exchange", (0, 2)),
        ("arrived<exchange", (1, 2)),
        ("exchange", 2),
        ("compress", 1),
        ("compress<beams", 1),
        ("send", 0),
        ("beams", 3),
        ("exchange", 3),
        ("beams<compress", (3, 2)),
        ("compress", 2),
        ("compress<own", 3),
        ("own", 3),
        ("compress", 3),
        ("send", 1),
        ("doppler", 0),
        ("doppler", 1),
    ]


def on_device(echoes, steer, code, beam_order, dwell, code_len):
    tiles, owners = lax.axis_size("tile"), lax.axis_size("beam")
    columns = echoes.shape[2]
    beam_total = steer.shape[1]
    pulses = columns // G
    total = pulses * owners
    tile_beams = beam_total // tiles
    own = tile_beams // owners

    values = echoes.astype(jnp.float32)
    power = sum_over(jnp.sum(values * values, axis=(0, 2))[None, :], "beam")

    order, lens, limits = lookup(beam_order, code_len, dwell, tile_beams)
    at = (lax.axis_index("beam") * pulses)[None]
    table = jnp.asarray(phase_table(total).astype(jnp.bfloat16))

    groups = groups_of(G)
    chunks = [chunk for group in groups for chunk in group]
    owner_of = [index for index, group in enumerate(groups) for _ in group]
    firsts = [owner_of.index(index) for index in range(len(groups))]
    own_parts, others, ready, ahead, got, out = {}, {}, {}, {}, {}, None
    for kind, number in order_of(groups):
        if kind == "beams":
            gate, gates = chunks[number]
            with jax.named_scope("beams"):
                picks = tuple(range(1 if number in LATER and tiles > 1 else 0, tiles))
                parts = form_beams(
                    echoes, power, order, steer, G, gate, gates, total * G, tiles, number in STREAMED, picks,
                    9 if number < len(groups[0]) + 1 else 0,
                )
            if len(picks) < tiles:
                parts = [parts[-1], *parts[:-1]]
            own_parts[number], *others[number] = parts
        elif kind == "own":
            if tiles > 1 and number in LATER:
                with jax.named_scope("beams"):
                    own_parts[number] = pick_own(own_parts[number], order, tiles)
        elif kind == "exchange":
            with jax.named_scope("tile_sum"):
                others[number] = [
                    lax.ppermute(part, "tile", [(i, (i + away) % tiles) for i in range(tiles)])
                    for away, part in enumerate(others[number], 1)
                ]
        elif kind == "arrived<exchange":
            others[number[0]][0], others[number[1]][0] = lax.optimization_barrier(
                (others[number[0]][0], others[number[1]][0])
            )
        elif kind == "compress":
            index = owner_of[number]
            place = number - firsts[index]
            with jax.named_scope("compress"):
                ready[index], ahead[number] = compress(
                    [own_parts[number]] + others[number],
                    ahead.get(number - 1), code, at, lens, limits, pulses, owners, number < len(chunks) - 1,
                    ready.get(index), len(groups[index]) - 1 - place, len(groups[index]), 100 if index else 3,
                )
        elif kind == "send":
            with jax.named_scope("to_owners"):
                got[number] = lax.all_to_all(ready[number], "beam", split_axis=0, concat_axis=0)
        elif kind == "doppler":
            with jax.named_scope("doppler"):
                out = doppler(got[number], table, out, groups[number][-1][0], pulses)
        elif kind == "beams<beams":
            power, own_parts[number] = lax.optimization_barrier((power, own_parts[number]))
        elif kind == "beams<compress":
            own_parts[number[1]], own_parts[number[0]] = lax.optimization_barrier(
                (own_parts[number[1]], own_parts[number[0]])
            )
        elif kind == "arrived<beams":
            power, others[number][0] = lax.optimization_barrier((power, others[number][0]))
        elif kind == "arrived<doppler":
            table, others[number][0] = lax.optimization_barrier((table, others[number][0]))
        elif kind == "compress<own":
            own_parts[number], ahead = lax.optimization_barrier((own_parts[number], ahead))
        elif kind == "compress<exchange":
            index = owner_of[number[0]]
            others[number[1]][0], ready[index] = lax.optimization_barrier((others[number[1]][0], ready[index]))
        elif kind == "compress<beams":
            index = owner_of[number]
            power, ready[index] = lax.optimization_barrier((power, ready[index]))
        elif kind == "compress<doppler":
            table, ahead[number] = lax.optimization_barrier((table, ahead[number]))
        elif kind == "doppler<compress":
            ahead[number], out = lax.optimization_barrier((ahead[number], out))
        elif kind == "last<doppler":
            out, ready[number] = lax.optimization_barrier((out, ready[number]))
    return out


def solution(mesh):
    placed = (P(None, "tile", "beam"), P(None, None, "tile"), P(), P(), P(), P())
    return jax.shard_map(
        on_device,
        mesh=mesh,
        in_specs=placed,
        out_specs=P(("tile", "beam"), None, None, None),
        check_vma=False,
    )
```

```python
import functools
import math

import jax
import jax.numpy as jnp
import numpy as np
from jax import lax
from jax.experimental import pallas as pl
from jax.experimental.pallas import tpu as pltpu
from jax.sharding import PartitionSpec as P

G = 32
EPS = 1e-05
CHUNK = 8
TOGETHER = (2, 2)
STREAMED = (0, 1, 3)
LATER = (0, 3)
NT = (((1,), (1,)), ((), ()))
TN = (((0,), (0,)), ((), ()))
MIB = 1024 * 1024


def params(mib):
    return pltpu.CompilerParams(vmem_limit_bytes=mib * MIB)


def busy(micros):
    return pl.CostEstimate(flops=int(micros * 1.15e9), bytes_accessed=1, transcendentals=0)


def block_of(size, most):
    return max(n for n in range(1, min(size, most) + 1) if size % n == 0)


def groups_of(gates):
    if CHUNK * sum(TOGETHER) != gates:
        return [[(0, gates)]]
    found, end = [], gates
    for count in TOGETHER:
        found.append([(end - CHUNK * (i + 1), CHUNK) for i in range(count)])
        end -= CHUNK * count
    return found


def in_hbm(*values):
    return [pltpu.with_memory_space_constraint(x, pltpu.HBM) for x in values]


def lookup_kernel(order_ref, lens_ref, limits_ref, near_ref, len_ref, limit_ref):
    tiles, mine = lax.axis_size("tile"), lax.axis_index("tile")
    beam_total, slots = order_ref.shape[1], len_ref.shape[1]
    for away in range(tiles):
        start = pl.multiple_of(lax.rem(mine + away, tiles) * slots, slots)
        near_ref[:, away * slots : (away + 1) * slots] = order_ref[:, pl.ds(start, slots)]
    wide = block_of(beam_total, 512)
    found = jnp.zeros((8, slots), jnp.float32)
    for first in range(0, beam_total, wide):
        at = slice(first, first + wide)
        lens, limits = lens_ref[:, at], limits_ref[:, at]
        row = lax.broadcasted_iota(jnp.int32, (8, wide), 0)
        values = jnp.where(row == 0, lens, jnp.where(row == 1, limits >> 5, limits & 31))
        beam = first + lax.broadcasted_iota(jnp.int32, (wide, slots), 0)
        pick = jnp.where(beam == near_ref[:, :slots], 1.0, 0.0).astype(jnp.bfloat16)
        found += jnp.dot(
            values.astype(jnp.float32).astype(jnp.bfloat16), pick, preferred_element_type=jnp.float32
        )
    found = found.astype(jnp.int32)
    len_ref[...] = found[0:1]
    limit_ref[...] = found[1:2] * 32 + found[2:3]


def lookup(order, code_len, dwell, slots):
    whole = pl.BlockSpec(memory_space=pltpu.VMEM)
    return pl.pallas_call(
        lookup_kernel,
        in_specs=[whole] * 3,
        out_specs=[whole] * 3,
        out_shape=[jax.ShapeDtypeStruct((1, size), jnp.int32) for size in (order.shape[0], slots, slots)],
        compiler_params=params(8),
        cost_estimate=busy(20),
        name="lookup",
    )(order[None, :], code_len[None, :], dwell[None, :])


def add_kernel(*refs):
    total = refs[0][...]
    for ref in refs[1:-1]:
        total = total + ref[...]
    refs[-1][...] = total


def add(*values):
    whole = pl.BlockSpec(memory_space=pltpu.VMEM)
    return pl.pallas_call(
        add_kernel,
        in_specs=[whole] * len(values),
        out_specs=whole,
        out_shape=jax.ShapeDtypeStruct(values[0].shape, values[0].dtype),
        compiler_params=params(1),
        cost_estimate=busy(1),
        name="add",
    )(*values)


def beam_kernel(samples, gates, gate, count, streamed, tiles, picks, echoes_ref, power_ref, order_ref, steer_ref, *rest):
    if streamed:
        steer_hbm, steer_ref, sem = steer_ref, rest[-2], rest[-1]
        rest = rest[:-2]
    out_refs, (scaled_ref, row_ref, picked_ref) = rest[:-3], rest[-3:]
    if len(picks) < tiles:
        *out_refs, beams_ref = out_refs
    _, chans, columns = echoes_ref.shape
    beam_total, wide = steer_ref.shape[1], row_ref.shape[0]
    steps = beam_total // wide

    def copy(part, step):
        at = pl.ds(step * wide, wide)
        return pltpu.make_async_copy(steer_hbm.at[part, at], steer_ref.at[part, at], sem.at[part, step])

    if streamed:
        for part in range(2):
            copy(part, 0).start()
    pulses = columns // gates
    rows = count * pulses
    row = lax.broadcasted_iota(jnp.int32, (rows, columns), 0)
    col = lax.broadcasted_iota(jnp.int32, (rows, columns), 1)
    source = (row % pulses) * gates + row // pulses + gate
    moved = jnp.where(source == col, 1.0, 0.0).astype(jnp.bfloat16)
    row_ref[...] = lax.broadcasted_iota(jnp.int32, row_ref.shape, 0)
    gain = lax.rsqrt(power_ref[...] / samples + EPS)
    real = lax.dot_general(moved, echoes_ref[0], NT, preferred_element_type=jnp.float32) * gain
    imag = lax.dot_general(moved, echoes_ref[1], NT, preferred_element_type=jnp.float32) * gain
    scaled_ref[:rows, :chans] = real.astype(jnp.bfloat16)
    scaled_ref[:rows, chans:] = (-imag).astype(jnp.bfloat16)
    scaled_ref[rows:, :chans] = imag.astype(jnp.bfloat16)
    scaled_ref[rows:, chans:] = real.astype(jnp.bfloat16)

    if streamed and steps > 1:
        for part in range(2):
            copy(part, 1).start()
    slots, tile_beams = row_ref.shape[1], beam_total // tiles
    starts = [start for tile in picks for start in range(tile * tile_beams, (tile + 1) * tile_beams, slots)]
    for step in range(steps):
        at = slice(step * wide, (step + 1) * wide)
        if streamed:
            for part in range(2):
                copy(part, step).wait()
                if step + 2 < steps:
                    copy(part, step + 2).start()
        beams = lax.dot_general(scaled_ref[:, :chans], steer_ref[0, at], NT, preferred_element_type=jnp.float32)
        beams += lax.dot_general(scaled_ref[:, chans:], steer_ref[1, at], NT, preferred_element_type=jnp.float32)
        beams = beams.astype(jnp.bfloat16)
        if len(picks) < tiles:
            beams_ref[:, at] = beams
        for start in starts:
            wanted = order_ref[:, start : start + slots] - step * wide
            pick = jnp.where(row_ref[...] == wanted, 1.0, 0.0).astype(jnp.bfloat16)
            picked = jnp.dot(beams, pick, preferred_element_type=jnp.float32)
            if step > 0:
                picked += picked_ref[:, start : start + slots]
            picked_ref[:, start : start + slots] = picked

    for tile, out_ref in zip(picks, out_refs):
        out_ref[...] = picked_ref[:, tile * tile_beams : (tile + 1) * tile_beams].astype(jnp.bfloat16)


def own_kernel(beams_ref, order_ref, out_ref, row_ref):
    beam_total, slots = beams_ref.shape[1], out_ref.shape[1]
    wide, some = row_ref.shape
    row_ref[...] = lax.broadcasted_iota(jnp.int32, row_ref.shape, 0)
    for start in range(0, slots, some):
        picked = None
        for first in range(0, beam_total, wide):
            wanted = order_ref[:, start : start + some] - first
            pick = jnp.where(row_ref[...] == wanted, 1.0, 0.0).astype(jnp.bfloat16)
            term = jnp.dot(beams_ref[:, first : first + wide], pick, preferred_element_type=jnp.float32)
            picked = term if picked is None else picked + term
        out_ref[:, start : start + some] = picked.astype(jnp.bfloat16)


def pick_own(beams, order, tiles):
    rows, beam_total = beams.shape
    slots = beam_total // tiles
    whole = pl.BlockSpec(memory_space=pltpu.VMEM)
    return pl.pallas_call(
        own_kernel,
        in_specs=[whole] * 2,
        out_specs=whole,
        out_shape=pltpu.VMEM((rows, slots), jnp.bfloat16),
        scratch_shapes=[pltpu.VMEM((block_of(beam_total, 512), block_of(slots, 512)), jnp.int32)],
        compiler_params=params(16),
        cost_estimate=busy(2),
        name="own",
    )(pltpu.with_memory_space_constraint(beams, pltpu.VMEM), order)


def form_beams(echoes, power, order, steer, gates, gate, count, samples, tiles, streamed, picks, micros):
    _, chans, columns = echoes.shape
    beam_total = steer.shape[1]
    tile_beams = beam_total // tiles
    rows = columns // gates * count
    wide = block_of(beam_total, 512)
    echoes = pltpu.with_memory_space_constraint(echoes, pltpu.VMEM)
    steer = pltpu.with_memory_space_constraint(steer, pltpu.HBM if streamed else pltpu.VMEM)
    whole = pl.BlockSpec(memory_space=pltpu.VMEM)
    spaces = [pltpu.HBM if tile else pltpu.VMEM for tile in picks]
    out_shape = [space((2 * rows, tile_beams), jnp.bfloat16) for space in spaces]
    if len(picks) < tiles:
        out_shape.append(pltpu.VMEM((2 * rows, beam_total), jnp.bfloat16))
    return pl.pallas_call(
        functools.partial(beam_kernel, samples, gates, gate, count, streamed, tiles, picks),
        in_specs=[whole] * 3 + [pl.BlockSpec(memory_space=pl.ANY) if streamed else whole],
        out_specs=[whole] * len(out_shape),
        out_shape=out_shape,
        scratch_shapes=[
            pltpu.VMEM((2 * rows, 2 * chans), jnp.bfloat16),
            pltpu.VMEM((wide, block_of(tile_beams, 512)), jnp.int32),
            pltpu.VMEM((2 * rows, beam_total), jnp.float32),
        ]
        + ([pltpu.VMEM(steer.shape, steer.dtype), pltpu.SemaphoreType.DMA((2, beam_total // wide))] if streamed else []),
        compiler_params=params(24),
        cost_estimate=busy(micros),
        name="beams",
    )(echoes, power, order, steer)


def factors_of(code_ref, lens, taps):
    return [
        tuple(
            jnp.where(tap < lens, code_ref[part : part + 1, tap : tap + 1].astype(jnp.float32), 0.0)
            for part in range(2)
        )
        for tap in range(taps)
    ]


def add_tap(real, imag, factor, shift_re, shift_im):
    code_re, code_im = factor
    term_re = code_re * shift_re + code_im * shift_im
    term_im = code_re * shift_im - code_im * shift_re
    return (term_re, term_im) if real is None else (real + term_re, imag + term_im)


def edge_kernel(pulses, taps, lanes, code_ref, lens_ref, ahead_ref, sums_ref):
    for first in range(0, lens_ref.shape[1], lanes):
        at = slice(first, first + lanes)
        factors = factors_of(code_ref, lens_ref[:, at], taps)
        after = [
            [ahead_ref[part, i * pulses : (i + 1) * pulses, at].astype(jnp.float32) for part in range(2)]
            for i in range(taps - 1)
        ]
        for gate in range(taps - 1):
            real = imag = None
            for i in range(gate + 1):
                real, imag = add_tap(real, imag, factors[taps - 1 - gate + i], *after[i])
            sums_ref[0, gate * pulses : (gate + 1) * pulses, at] = real
            sums_ref[1, gate * pulses : (gate + 1) * pulses, at] = imag


def edge_sums(ahead, code, lens, pulses):
    whole = pl.BlockSpec(memory_space=pltpu.VMEM)
    return pl.pallas_call(
        functools.partial(edge_kernel, pulses, code.shape[1], block_of(lens.shape[1], 256)),
        in_specs=[whole] * 3,
        out_specs=whole,
        out_shape=pltpu.VMEM(ahead.shape, jnp.float32),
        compiler_params=params(16),
        cost_estimate=busy(1),
        name="edge",
    )(code, lens, pltpu.with_memory_space_constraint(ahead, pltpu.VMEM))


def compress_kernel(pulses, taps, parts_in, halo, shared, keep_ahead, place, code_ref, at_ref, lens_ref, limits_ref, *rest):
    part_refs, rest = rest[:parts_in], rest[parts_in:]
    if halo:
        sums_ref, rest = rest[0], rest[1:]
    out_hbm, rest = rest[shared], rest[shared + 1 :]
    away = keep_ahead and place == 0
    if away:
        beams_hbm, beams_ref, beams_sem, rest = rest[0], rest[-2], rest[-1], rest[1:-2]
    elif keep_ahead:
        beams_ref, rest = rest[0], rest[1:]
    wide_ref, laid_ref, sem = rest
    rows, tile_beams = part_refs[0].shape[0] // 2, part_refs[0].shape[1]
    edge = (taps - 1) * pulses
    lanes = wide_ref.shape[2]
    own = laid_ref.shape[2] // 2
    some = lanes // own

    def copy(block):
        at = pl.ds(block * some, some)
        return pltpu.make_async_copy(
            laid_ref.at[at], out_hbm.at[at, pl.ds(place * rows, rows)], sem.at[block]
        )

    def beams_copy(block):
        at = pl.ds(block * lanes, lanes)
        return pltpu.make_async_copy(beams_ref.at[:, :, at], beams_hbm.at[:, :, at], beams_sem.at[block])

    for block in range(tile_beams // lanes):
        at = slice(block * lanes, (block + 1) * lanes)
        for part in range(2):
            total = part_refs[0][part * rows : (part + 1) * rows, at].astype(jnp.float32)
            for ref in part_refs[1:]:
                total += ref[part * rows : (part + 1) * rows, at].astype(jnp.float32)
            rounded = total.astype(jnp.bfloat16)
            if keep_ahead:
                beams_ref[part, :, at] = rounded[:edge]
            wide_ref[part] = rounded.astype(jnp.float32)
        if away:
            beams_copy(block).start()
        lens, limits = lens_ref[:, at], limits_ref[:, at]
        pulse = at_ref[0] + lax.broadcasted_iota(jnp.int32, (pulses, lanes), 0)
        keep = pulse < limits
        factors = factors_of(code_ref, lens, taps)
        gates = rows // pulses
        for gate in range(gates):
            real = imag = None
            before = gate - (gates - taps + 1)
            if halo and before >= 0:
                real = sums_ref[0, before * pulses : (before + 1) * pulses, at]
                imag = sums_ref[1, before * pulses : (before + 1) * pulses, at]
            for tap in range(min(taps, gates - gate)):
                start = (gate + tap) * pulses
                real, imag = add_tap(
                    real, imag, factors[tap], wide_ref[0, start : start + pulses], wide_ref[1, start : start + pulses]
                )
            real = jnp.where(keep, real, 0.0)
            imag = jnp.where(keep, imag, 0.0)
            for owner in range(some):
                line = slice(owner * own, (owner + 1) * own)
                joined = jnp.concatenate([real[:, line], imag[:, line]], axis=1).astype(jnp.bfloat16)
                laid_ref[block * some + owner, gate * pulses : (gate + 1) * pulses] = joined
        copy(block).start()
    for block in range(tile_beams // lanes):
        copy(block).wait()
        if away:
            beams_copy(block).wait()


def compress(parts, ahead, code, at, lens, limits, pulses, owners, keep_ahead, ready, place, places, micros):
    taps = code.shape[1]
    rows, tile_beams = parts[0].shape[0] // 2, parts[0].shape[1]
    own = tile_beams // owners
    lanes = block_of(tile_beams, 256)
    edge = (taps - 1) * pulses
    whole, apart = pl.BlockSpec(memory_space=pltpu.VMEM), pl.BlockSpec(memory_space=pl.ANY)
    scalars = pl.BlockSpec(memory_space=pltpu.SMEM)
    out_shape = [pltpu.HBM((owners, places * rows, 2 * own), jnp.bfloat16)]
    if keep_ahead:
        out_shape.append((pltpu.VMEM if place else pltpu.HBM)((2, edge, tile_beams), jnp.bfloat16))
    near = [pltpu.with_memory_space_constraint(x, pltpu.VMEM) for x in parts + ([] if ahead is None else [ahead])]
    shared = [] if ready is None else in_hbm(ready)
    done = pl.pallas_call(
        functools.partial(
            compress_kernel, pulses, taps, len(parts), ahead is not None, len(shared), keep_ahead, place
        ),
        in_specs=[whole, scalars, whole, whole] + [whole] * len(near) + [apart] * len(shared),
        out_specs=[apart] + [whole if place else apart] * keep_ahead,
        out_shape=out_shape,
        scratch_shapes=[
            pltpu.VMEM((2, rows, lanes), jnp.float32),
            pltpu.VMEM((owners, rows, 2 * own), jnp.bfloat16),
            pltpu.SemaphoreType.DMA((tile_beams // lanes,)),
        ]
        + (
            [pltpu.VMEM((2, edge, tile_beams), jnp.bfloat16), pltpu.SemaphoreType.DMA((tile_beams // lanes,))]
            if keep_ahead and place == 0
            else []
        ),
        input_output_aliases={4 + len(near): 0} if shared else {},
        compiler_params=params(16),
        cost_estimate=busy(micros),
        name="compress",
    )(code, at, lens, limits, *near, *shared)
    return done if keep_ahead else (done[0], None)


def doppler_kernel(pulses, first, some, got_ref, table_ref, *rest):
    out_hbm, lines_ref, block_ref, sem = rest[-4:]
    owners, rows, lanes = got_ref.shape
    own, bins = lanes // 2, table_ref.shape[1] // 2
    gates = rows // pulses
    batch = block_of(some, max(1, 512 // lanes))

    def copy(block):
        at = pl.ds(first + block * some, some)
        return pltpu.make_async_copy(block_ref.at[block], out_hbm.at[:, :, at], sem.at[block])

    for block in range(gates // some):
        for start in range(0, some, batch):
            values = jnp.concatenate(
                [
                    got_ref[:, gate * pulses : (gate + 1) * pulses].reshape(owners * pulses, lanes)
                    for gate in range(block * some + start, block * some + start + batch)
                ],
                axis=1,
            )
            both = lax.dot_general(values, table_ref[...], TN, preferred_element_type=jnp.float32)
            for index in range(batch):
                upper = both[index * lanes : index * lanes + own]
                lower = both[index * lanes + own : (index + 1) * lanes]
                real = upper[:, :bins] - lower[:, bins:]
                imag = lower[:, :bins] + upper[:, bins:]
                for part, line in enumerate((real, imag)):
                    for at in range(lines_ref.shape[0]):
                        to = pl.ds(part * some + start + index, own, stride=2 * some)
                        lines_ref[at, to, :] = line[:, at * 128 : (at + 1) * 128]
        for at in range(lines_ref.shape[0]):
            block_ref[block, :, :, :, at * 128 : (at + 1) * 128] = lines_ref[at].reshape(own, 2, some, 128)
        copy(block).start()
    for block in range(gates // some):
        copy(block).wait()


def doppler(got, table, out, first, pulses):
    owners, rows, lanes = got.shape
    own, bins, gates = lanes // 2, table.shape[1] // 2, rows // pulses
    some = CHUNK if gates % CHUNK == 0 else gates
    whole, apart = pl.BlockSpec(memory_space=pltpu.VMEM), pl.BlockSpec(memory_space=pl.ANY)
    before = [] if out is None else [out]
    return pl.pallas_call(
        functools.partial(doppler_kernel, pulses, first, some),
        in_specs=[whole, whole] + [apart] * len(before),
        out_specs=apart,
        out_shape=jax.ShapeDtypeStruct((own, 2, G, bins), jnp.float32),
        scratch_shapes=[
            pltpu.VMEM((bins // 128, own * 2 * some, 128), jnp.float32),
            pltpu.VMEM((gates // some, own, 2, some, bins), jnp.float32),
            pltpu.SemaphoreType.DMA((gates // some,)),
        ],
        input_output_aliases={2: 0} if before else {},
        compiler_params=params(24),
        cost_estimate=busy(3),
        name="doppler",
    )(pltpu.with_memory_space_constraint(got, pltpu.VMEM), table, *before)


def phase_table(total):
    angle = np.outer(np.arange(total), np.arange(total)) % total * (2.0 * math.pi / total)
    return np.concatenate([np.cos(angle), -np.sin(angle)], axis=1) / math.sqrt(total)


def sum_over(values, axis):
    size = lax.axis_size(axis)
    if size & (size - 1):
        return lax.psum(values, axis)
    step = 1
    while step < size:
        steps = [step * i for i in (1, 2, 3) if step * i < size] if step * 2 < size else [step]
        values = add(
            values, *(lax.ppermute(values, axis, [(i, i ^ away) for i in range(size)]) for away in steps)
        )
        step *= len(steps) + 1
    return values


def order_of(groups):
    count = sum(len(group) for group in groups)
    if count == 1:
        return [("beams", 0), ("exchange", 0), ("own", 0), ("compress", 0), ("send", 0), ("doppler", 0)]
    return [
        ("beams", 0),
        ("exchange", 0),
        ("beams<beams", 0),
        ("beams", 1),
        ("exchange", 1),
        ("beams<compress", (1, 0)),
        ("own", 0),
        ("beams<beams", 1),
        ("beams", 2),
        ("beams<compress", (2, 0)),
        ("compress", 0),
        ("compress<exchange", (0, 2)),
        ("arrived<exchange", (1, 2)),
        ("exchange", 2),
        ("compress", 1),
        ("compress<beams", 1),
        ("send", 0),
        ("beams", 3),
        ("exchange", 3),
        ("beams<compress", (3, 2)),
        ("compress", 2),
        ("compress<own", 3),
        ("own", 3),
        ("compress", 3),
        ("send", 1),
        ("doppler", 0),
        ("doppler", 1),
    ]


def on_device(echoes, steer, code, beam_order, dwell, code_len):
    tiles, owners = lax.axis_size("tile"), lax.axis_size("beam")
    columns = echoes.shape[2]
    beam_total = steer.shape[1]
    pulses = columns // G
    total = pulses * owners
    tile_beams = beam_total // tiles
    own = tile_beams // owners

    values = echoes.astype(jnp.float32)
    power = sum_over(jnp.sum(values * values, axis=(0, 2))[None, :], "beam")

    order, lens, limits = lookup(beam_order, code_len, dwell, tile_beams)
    at = (lax.axis_index("beam") * pulses)[None]
    table = jnp.asarray(phase_table(total).astype(jnp.bfloat16))

    groups = groups_of(G)
    chunks = [chunk for group in groups for chunk in group]
    owner_of = [index for index, group in enumerate(groups) for _ in group]
    firsts = [owner_of.index(index) for index in range(len(groups))]
    own_parts, others, ready, ahead, got, out = {}, {}, {}, {}, {}, None
    for kind, number in order_of(groups):
        if kind == "beams":
            gate, gates = chunks[number]
            with jax.named_scope("beams"):
                picks = tuple(range(1 if number in LATER and tiles > 1 else 0, tiles))
                parts = form_beams(
                    echoes, power, order, steer, G, gate, gates, total * G, tiles, number in STREAMED, picks,
                    9 if number < len(groups[0]) + 1 else 0,
                )
            if len(picks) < tiles:
                parts = [parts[-1], *parts[:-1]]
            own_parts[number], *others[number] = parts
        elif kind == "own":
            if tiles > 1 and number in LATER:
                with jax.named_scope("beams"):
                    own_parts[number] = pick_own(own_parts[number], order, tiles)
        elif kind == "exchange":
            with jax.named_scope("tile_sum"):
                others[number] = [
                    lax.ppermute(part, "tile", [(i, (i + away) % tiles) for i in range(tiles)])
                    for away, part in enumerate(others[number], 1)
                ]
        elif kind == "arrived<exchange":
            others[number[0]][0], others[number[1]][0] = lax.optimization_barrier(
                (others[number[0]][0], others[number[1]][0])
            )
        elif kind == "compress":
            index = owner_of[number]
            place = number - firsts[index]
            with jax.named_scope("compress"):
                ready[index], ahead[number] = compress(
                    [own_parts[number]] + others[number],
                    ahead.get(number - 1), code, at, lens, limits, pulses, owners, number < len(chunks) - 1,
                    ready.get(index), len(groups[index]) - 1 - place, len(groups[index]), 100 if index else 3,
                )
            if ahead[number] is not None:
                with jax.named_scope("edge"):
                    ahead[number] = edge_sums(ahead[number], code, lens, pulses)
        elif kind == "send":
            with jax.named_scope("to_owners"):
                got[number] = lax.all_to_all(ready[number], "beam", split_axis=0, concat_axis=0)
        elif kind == "doppler":
            with jax.named_scope("doppler"):
                out = doppler(got[number], table, out, groups[number][-1][0], pulses)
        elif kind == "beams<beams":
            power, own_parts[number] = lax.optimization_barrier((power, own_parts[number]))
        elif kind == "beams<compress":
            own_parts[number[1]], own_parts[number[0]] = lax.optimization_barrier(
                (own_parts[number[1]], own_parts[number[0]])
            )
        elif kind == "arrived<beams":
            power, others[number][0] = lax.optimization_barrier((power, others[number][0]))
        elif kind == "arrived<doppler":
            table, others[number][0] = lax.optimization_barrier((table, others[number][0]))
        elif kind == "compress<own":
            own_parts[number], ahead = lax.optimization_barrier((own_parts[number], ahead))
        elif kind == "compress<exchange":
            others[number[1]][0], ahead[number[0]] = lax.optimization_barrier(
                (others[number[1]][0], ahead[number[0]])
            )
        elif kind == "compress<beams":
            index = owner_of[number]
            power, ready[index] = lax.optimization_barrier((power, ready[index]))
        elif kind == "compress<doppler":
            table, ahead[number] = lax.optimization_barrier((table, ahead[number]))
        elif kind == "doppler<compress":
            ahead[number], out = lax.optimization_barrier((ahead[number], out))
        elif kind == "last<doppler":
            out, ready[number] = lax.optimization_barrier((out, ready[number]))
    return out


def solution(mesh):
    placed = (P(None, "tile", "beam"), P(None, None, "tile"), P(), P(), P(), P())
    return jax.shard_map(
        on_device,
        mesh=mesh,
        in_specs=placed,
        out_specs=P(("tile", "beam"), None, None, None),
        check_vma=False,
    )
```

```python
import functools
import math

import jax
import jax.numpy as jnp
import numpy as np
from jax import lax
from jax.experimental import pallas as pl
from jax.experimental.pallas import tpu as pltpu
from jax.sharding import PartitionSpec as P

G = 32
EPS = 1e-05
CHUNK = 8
TOGETHER = (2, 2)
STREAMED = (0, 1, 3)
LATER = (0, 3)
NT = (((1,), (1,)), ((), ()))
TN = (((0,), (0,)), ((), ()))
MIB = 1024 * 1024


def params(mib):
    return pltpu.CompilerParams(vmem_limit_bytes=mib * MIB)


def busy(micros):
    return pl.CostEstimate(flops=int(micros * 1.15e9), bytes_accessed=1, transcendentals=0)


def block_of(size, most):
    return max(n for n in range(1, min(size, most) + 1) if size % n == 0)


def groups_of(gates):
    if CHUNK * sum(TOGETHER) != gates:
        return [[(0, gates)]]
    found, end = [], gates
    for count in TOGETHER:
        found.append([(end - CHUNK * (i + 1), CHUNK) for i in range(count)])
        end -= CHUNK * count
    return found


def in_hbm(*values):
    return [pltpu.with_memory_space_constraint(x, pltpu.HBM) for x in values]


def lookup_kernel(order_ref, lens_ref, limits_ref, near_ref, len_ref, limit_ref):
    tiles, mine = lax.axis_size("tile"), lax.axis_index("tile")
    beam_total, slots = order_ref.shape[1], len_ref.shape[1]
    for away in range(tiles):
        start = pl.multiple_of(lax.rem(mine + away, tiles) * slots, slots)
        near_ref[:, away * slots : (away + 1) * slots] = order_ref[:, pl.ds(start, slots)]
    wide = block_of(beam_total, 512)
    found = jnp.zeros((8, slots), jnp.float32)
    for first in range(0, beam_total, wide):
        at = slice(first, first + wide)
        lens, limits = lens_ref[:, at], limits_ref[:, at]
        row = lax.broadcasted_iota(jnp.int32, (8, wide), 0)
        values = jnp.where(row == 0, lens, jnp.where(row == 1, limits >> 5, limits & 31))
        beam = first + lax.broadcasted_iota(jnp.int32, (wide, slots), 0)
        pick = jnp.where(beam == near_ref[:, :slots], 1.0, 0.0).astype(jnp.bfloat16)
        found += jnp.dot(
            values.astype(jnp.float32).astype(jnp.bfloat16), pick, preferred_element_type=jnp.float32
        )
    found = found.astype(jnp.int32)
    len_ref[...] = found[0:1]
    limit_ref[...] = found[1:2] * 32 + found[2:3]


def lookup(order, code_len, dwell, slots):
    whole = pl.BlockSpec(memory_space=pltpu.VMEM)
    return pl.pallas_call(
        lookup_kernel,
        in_specs=[whole] * 3,
        out_specs=[whole] * 3,
        out_shape=[jax.ShapeDtypeStruct((1, size), jnp.int32) for size in (order.shape[0], slots, slots)],
        compiler_params=params(8),
        cost_estimate=busy(20),
        name="lookup",
    )(order[None, :], code_len[None, :], dwell[None, :])


def add_kernel(*refs):
    total = refs[0][...]
    for ref in refs[1:-1]:
        total = total + ref[...]
    refs[-1][...] = total


def add(*values):
    whole = pl.BlockSpec(memory_space=pltpu.VMEM)
    return pl.pallas_call(
        add_kernel,
        in_specs=[whole] * len(values),
        out_specs=whole,
        out_shape=jax.ShapeDtypeStruct(values[0].shape, values[0].dtype),
        compiler_params=params(1),
        cost_estimate=busy(1),
        name="add",
    )(*values)


def beam_kernel(samples, gates, gate, count, streamed, tiles, picks, echoes_ref, power_ref, order_ref, steer_ref, *rest):
    if streamed:
        steer_hbm, steer_ref, sem = steer_ref, rest[-2], rest[-1]
        rest = rest[:-2]
    out_refs, (scaled_ref, row_ref, picked_ref) = rest[:-3], rest[-3:]
    if len(picks) < tiles:
        *out_refs, beams_ref = out_refs
    _, chans, columns = echoes_ref.shape
    beam_total, wide = steer_ref.shape[1], row_ref.shape[0]
    steps = beam_total // wide

    def copy(part, step):
        at = pl.ds(step * wide, wide)
        return pltpu.make_async_copy(steer_hbm.at[part, at], steer_ref.at[part, at], sem.at[part, step])

    if streamed:
        for part in range(2):
            copy(part, 0).start()
    pulses = columns // gates
    rows = count * pulses
    row = lax.broadcasted_iota(jnp.int32, (rows, columns), 0)
    col = lax.broadcasted_iota(jnp.int32, (rows, columns), 1)
    source = (row % pulses) * gates + row // pulses + gate
    moved = jnp.where(source == col, 1.0, 0.0).astype(jnp.bfloat16)
    row_ref[...] = lax.broadcasted_iota(jnp.int32, row_ref.shape, 0)
    gain = lax.rsqrt(power_ref[...] / samples + EPS)
    real = lax.dot_general(moved, echoes_ref[0], NT, preferred_element_type=jnp.float32) * gain
    imag = lax.dot_general(moved, echoes_ref[1], NT, preferred_element_type=jnp.float32) * gain
    scaled_ref[:rows, :chans] = real.astype(jnp.bfloat16)
    scaled_ref[:rows, chans:] = (-imag).astype(jnp.bfloat16)
    scaled_ref[rows:, :chans] = imag.astype(jnp.bfloat16)
    scaled_ref[rows:, chans:] = real.astype(jnp.bfloat16)

    if streamed and steps > 1:
        for part in range(2):
            copy(part, 1).start()
    slots, tile_beams = row_ref.shape[1], beam_total // tiles
    starts = [start for tile in picks for start in range(tile * tile_beams, (tile + 1) * tile_beams, slots)]
    for step in range(steps):
        at = slice(step * wide, (step + 1) * wide)
        if streamed:
            for part in range(2):
                copy(part, step).wait()
                if step + 2 < steps:
                    copy(part, step + 2).start()
        beams = lax.dot_general(scaled_ref[:, :chans], steer_ref[0, at], NT, preferred_element_type=jnp.float32)
        beams += lax.dot_general(scaled_ref[:, chans:], steer_ref[1, at], NT, preferred_element_type=jnp.float32)
        beams = beams.astype(jnp.bfloat16)
        if len(picks) < tiles:
            beams_ref[:, at] = beams
        for start in starts:
            wanted = order_ref[:, start : start + slots] - step * wide
            pick = jnp.where(row_ref[...] == wanted, 1.0, 0.0).astype(jnp.bfloat16)
            picked = jnp.dot(beams, pick, preferred_element_type=jnp.float32)
            if step > 0:
                picked += picked_ref[:, start : start + slots]
            picked_ref[:, start : start + slots] = picked

    for tile, out_ref in zip(picks, out_refs):
        out_ref[...] = picked_ref[:, tile * tile_beams : (tile + 1) * tile_beams].astype(jnp.bfloat16)


def own_kernel(beams_ref, order_ref, out_ref, row_ref):
    beam_total, slots = beams_ref.shape[1], out_ref.shape[1]
    wide, some = row_ref.shape
    row_ref[...] = lax.broadcasted_iota(jnp.int32, row_ref.shape, 0)
    for start in range(0, slots, some):
        picked = None
        for first in range(0, beam_total, wide):
            wanted = order_ref[:, start : start + some] - first
            pick = jnp.where(row_ref[...] == wanted, 1.0, 0.0).astype(jnp.bfloat16)
            term = jnp.dot(beams_ref[:, first : first + wide], pick, preferred_element_type=jnp.float32)
            picked = term if picked is None else picked + term
        out_ref[:, start : start + some] = picked.astype(jnp.bfloat16)


def pick_own(beams, order, tiles):
    rows, beam_total = beams.shape
    slots = beam_total // tiles
    whole = pl.BlockSpec(memory_space=pltpu.VMEM)
    return pl.pallas_call(
        own_kernel,
        in_specs=[whole] * 2,
        out_specs=whole,
        out_shape=pltpu.VMEM((rows, slots), jnp.bfloat16),
        scratch_shapes=[pltpu.VMEM((block_of(beam_total, 512), block_of(slots, 512)), jnp.int32)],
        compiler_params=params(16),
        cost_estimate=busy(2),
        name="own",
    )(pltpu.with_memory_space_constraint(beams, pltpu.VMEM), order)


def form_beams(echoes, power, order, steer, gates, gate, count, samples, tiles, streamed, picks, micros):
    _, chans, columns = echoes.shape
    beam_total = steer.shape[1]
    tile_beams = beam_total // tiles
    rows = columns // gates * count
    wide = block_of(beam_total, 512)
    echoes = pltpu.with_memory_space_constraint(echoes, pltpu.VMEM)
    steer = pltpu.with_memory_space_constraint(steer, pltpu.HBM if streamed else pltpu.VMEM)
    whole = pl.BlockSpec(memory_space=pltpu.VMEM)
    spaces = [pltpu.HBM if tile else pltpu.VMEM for tile in picks]
    out_shape = [space((2 * rows, tile_beams), jnp.bfloat16) for space in spaces]
    if len(picks) < tiles:
        out_shape.append(pltpu.VMEM((2 * rows, beam_total), jnp.bfloat16))
    return pl.pallas_call(
        functools.partial(beam_kernel, samples, gates, gate, count, streamed, tiles, picks),
        in_specs=[whole] * 3 + [pl.BlockSpec(memory_space=pl.ANY) if streamed else whole],
        out_specs=[whole] * len(out_shape),
        out_shape=out_shape,
        scratch_shapes=[
            pltpu.VMEM((2 * rows, 2 * chans), jnp.bfloat16),
            pltpu.VMEM((wide, block_of(tile_beams, 512)), jnp.int32),
            pltpu.VMEM((2 * rows, beam_total), jnp.float32),
        ]
        + ([pltpu.VMEM(steer.shape, steer.dtype), pltpu.SemaphoreType.DMA((2, beam_total // wide))] if streamed else []),
        compiler_params=params(24),
        cost_estimate=busy(micros),
        name="beams",
    )(echoes, power, order, steer)


def factors_of(code_ref, lens, taps):
    code = code_ref[...].astype(jnp.float32)
    return [
        tuple(jnp.where(tap < lens, code[part : part + 1, tap : tap + 1], 0.0) for part in range(2))
        for tap in range(taps)
    ]


def add_tap(real, imag, factor, shift_re, shift_im):
    code_re, code_im = factor
    term_re = code_re * shift_re + code_im * shift_im
    term_im = code_re * shift_im - code_im * shift_re
    return (term_re, term_im) if real is None else (real + term_re, imag + term_im)


def edge_kernel(pulses, taps, lanes, code_ref, lens_ref, ahead_ref, sums_ref):
    for first in range(0, lens_ref.shape[1], lanes):
        at = slice(first, first + lanes)
        factors = factors_of(code_ref, lens_ref[:, at], taps)
        after = [
            [ahead_ref[part, i * pulses : (i + 1) * pulses, at].astype(jnp.float32) for part in range(2)]
            for i in range(taps - 1)
        ]
        for gate in range(taps - 1):
            real = imag = None
            for i in range(gate + 1):
                real, imag = add_tap(real, imag, factors[taps - 1 - gate + i], *after[i])
            sums_ref[0, gate * pulses : (gate + 1) * pulses, at] = real
            sums_ref[1, gate * pulses : (gate + 1) * pulses, at] = imag


def edge_sums(ahead, code, lens, pulses):
    whole = pl.BlockSpec(memory_space=pltpu.VMEM)
    return pl.pallas_call(
        functools.partial(edge_kernel, pulses, code.shape[1], block_of(lens.shape[1], 256)),
        in_specs=[whole] * 3,
        out_specs=whole,
        out_shape=pltpu.VMEM(ahead.shape, jnp.float32),
        compiler_params=params(16),
        cost_estimate=busy(1),
        name="edge",
    )(code, lens, pltpu.with_memory_space_constraint(ahead, pltpu.VMEM))


def compress_kernel(pulses, taps, parts_in, halo, shared, keep_ahead, place, code_ref, at_ref, lens_ref, limits_ref, *rest):
    part_refs, rest = rest[:parts_in], rest[parts_in:]
    if halo:
        sums_ref, rest = rest[0], rest[1:]
    out_hbm, rest = rest[shared], rest[shared + 1 :]
    away = keep_ahead and place == 0
    if away:
        beams_hbm, beams_ref, beams_sem, rest = rest[0], rest[-2], rest[-1], rest[1:-2]
    elif keep_ahead:
        beams_ref, rest = rest[0], rest[1:]
    wide_ref, laid_ref, sem = rest
    rows, tile_beams = part_refs[0].shape[0] // 2, part_refs[0].shape[1]
    edge = (taps - 1) * pulses
    lanes = wide_ref.shape[2]
    own = laid_ref.shape[2] // 2
    some = lanes // own

    def copy(block):
        at = pl.ds(block * some, some)
        return pltpu.make_async_copy(
            laid_ref.at[at], out_hbm.at[at, pl.ds(place * rows, rows)], sem.at[block]
        )

    def beams_copy(block):
        at = pl.ds(block * lanes, lanes)
        return pltpu.make_async_copy(beams_ref.at[:, :, at], beams_hbm.at[:, :, at], beams_sem.at[block])

    for block in range(tile_beams // lanes):
        at = slice(block * lanes, (block + 1) * lanes)
        for part in range(2):
            total = part_refs[0][part * rows : (part + 1) * rows, at].astype(jnp.float32)
            for ref in part_refs[1:]:
                total += ref[part * rows : (part + 1) * rows, at].astype(jnp.float32)
            rounded = total.astype(jnp.bfloat16)
            if keep_ahead:
                beams_ref[part, :, at] = rounded[:edge]
            wide_ref[part] = rounded.astype(jnp.float32)
        if away:
            beams_copy(block).start()
        lens, limits = lens_ref[:, at], limits_ref[:, at]
        pulse = at_ref[0] + lax.broadcasted_iota(jnp.int32, (pulses, lanes), 0)
        keep = pulse < limits
        factors = factors_of(code_ref, lens, taps)
        gates = rows // pulses
        for gate in range(gates):
            real = imag = None
            before = gate - (gates - taps + 1)
            if halo and before >= 0:
                real = sums_ref[0, before * pulses : (before + 1) * pulses, at]
                imag = sums_ref[1, before * pulses : (before + 1) * pulses, at]
            for tap in range(min(taps, gates - gate)):
                start = (gate + tap) * pulses
                real, imag = add_tap(
                    real, imag, factors[tap], wide_ref[0, start : start + pulses], wide_ref[1, start : start + pulses]
                )
            real = jnp.where(keep, real, 0.0)
            imag = jnp.where(keep, imag, 0.0)
            for owner in range(some):
                line = slice(owner * own, (owner + 1) * own)
                joined = jnp.concatenate([real[:, line], imag[:, line]], axis=1).astype(jnp.bfloat16)
                laid_ref[block * some + owner, gate * pulses : (gate + 1) * pulses] = joined
        copy(block).start()
    for block in range(tile_beams // lanes):
        copy(block).wait()
        if away:
            beams_copy(block).wait()


def compress(parts, ahead, code, at, lens, limits, pulses, owners, keep_ahead, ready, place, places, micros):
    taps = code.shape[1]
    rows, tile_beams = parts[0].shape[0] // 2, parts[0].shape[1]
    own = tile_beams // owners
    lanes = block_of(tile_beams, 256)
    edge = (taps - 1) * pulses
    whole, apart = pl.BlockSpec(memory_space=pltpu.VMEM), pl.BlockSpec(memory_space=pl.ANY)
    scalars = pl.BlockSpec(memory_space=pltpu.SMEM)
    out_shape = [pltpu.HBM((owners, places * rows, 2 * own), jnp.bfloat16)]
    if keep_ahead:
        out_shape.append((pltpu.VMEM if place else pltpu.HBM)((2, edge, tile_beams), jnp.bfloat16))
    near = [pltpu.with_memory_space_constraint(x, pltpu.VMEM) for x in parts + ([] if ahead is None else [ahead])]
    shared = [] if ready is None else in_hbm(ready)
    done = pl.pallas_call(
        functools.partial(
            compress_kernel, pulses, taps, len(parts), ahead is not None, len(shared), keep_ahead, place
        ),
        in_specs=[whole, scalars, whole, whole] + [whole] * len(near) + [apart] * len(shared),
        out_specs=[apart] + [whole if place else apart] * keep_ahead,
        out_shape=out_shape,
        scratch_shapes=[
            pltpu.VMEM((2, rows, lanes), jnp.float32),
            pltpu.VMEM((owners, rows, 2 * own), jnp.bfloat16),
            pltpu.SemaphoreType.DMA((tile_beams // lanes,)),
        ]
        + (
            [pltpu.VMEM((2, edge, tile_beams), jnp.bfloat16), pltpu.SemaphoreType.DMA((tile_beams // lanes,))]
            if keep_ahead and place == 0
            else []
        ),
        input_output_aliases={4 + len(near): 0} if shared else {},
        compiler_params=params(16),
        cost_estimate=busy(micros),
        name="compress",
    )(code, at, lens, limits, *near, *shared)
    return done if keep_ahead else (done[0], None)


def doppler_kernel(pulses, first, some, got_ref, table_ref, *rest):
    out_hbm, lines_ref, block_ref, sem = rest[-4:]
    owners, rows, lanes = got_ref.shape
    own, bins = lanes // 2, table_ref.shape[1] // 2
    gates = rows // pulses
    batch = block_of(some, max(1, 512 // lanes))

    def copy(block):
        at = pl.ds(first + block * some, some)
        return pltpu.make_async_copy(block_ref.at[block], out_hbm.at[:, :, at], sem.at[block])

    for block in range(gates // some):
        for start in range(0, some, batch):
            values = jnp.concatenate(
                [
                    got_ref[:, gate * pulses : (gate + 1) * pulses].reshape(owners * pulses, lanes)
                    for gate in range(block * some + start, block * some + start + batch)
                ],
                axis=1,
            )
            both = lax.dot_general(values, table_ref[...], TN, preferred_element_type=jnp.float32)
            for index in range(batch):
                upper = both[index * lanes : index * lanes + own]
                lower = both[index * lanes + own : (index + 1) * lanes]
                real = upper[:, :bins] - lower[:, bins:]
                imag = lower[:, :bins] + upper[:, bins:]
                for part, line in enumerate((real, imag)):
                    for at in range(lines_ref.shape[0]):
                        to = pl.ds(part * some + start + index, own, stride=2 * some)
                        lines_ref[at, to, :] = line[:, at * 128 : (at + 1) * 128]
        for at in range(lines_ref.shape[0]):
            block_ref[block, :, :, :, at * 128 : (at + 1) * 128] = lines_ref[at].reshape(own, 2, some, 128)
        copy(block).start()
    for block in range(gates // some):
        copy(block).wait()


def doppler(got, table, out, first, pulses):
    owners, rows, lanes = got.shape
    own, bins, gates = lanes // 2, table.shape[1] // 2, rows // pulses
    some = CHUNK if gates % CHUNK == 0 else gates
    whole, apart = pl.BlockSpec(memory_space=pltpu.VMEM), pl.BlockSpec(memory_space=pl.ANY)
    before = [] if out is None else [out]
    return pl.pallas_call(
        functools.partial(doppler_kernel, pulses, first, some),
        in_specs=[whole, whole] + [apart] * len(before),
        out_specs=apart,
        out_shape=jax.ShapeDtypeStruct((own, 2, G, bins), jnp.float32),
        scratch_shapes=[
            pltpu.VMEM((bins // 128, own * 2 * some, 128), jnp.float32),
            pltpu.VMEM((gates // some, own, 2, some, bins), jnp.float32),
            pltpu.SemaphoreType.DMA((gates // some,)),
        ],
        input_output_aliases={2: 0} if before else {},
        compiler_params=params(24),
        cost_estimate=busy(3),
        name="doppler",
    )(pltpu.with_memory_space_constraint(got, pltpu.VMEM), table, *before)


def phase_table(total):
    angle = np.outer(np.arange(total), np.arange(total)) % total * (2.0 * math.pi / total)
    return np.concatenate([np.cos(angle), -np.sin(angle)], axis=1) / math.sqrt(total)


def sum_over(values, axis):
    size = lax.axis_size(axis)
    if size & (size - 1):
        return lax.psum(values, axis)
    step = 1
    while step < size:
        steps = [step * i for i in (1, 2, 3) if step * i < size] if step * 2 < size else [step]
        values = add(
            values, *(lax.ppermute(values, axis, [(i, i ^ away) for i in range(size)]) for away in steps)
        )
        step *= len(steps) + 1
    return values


def order_of(groups):
    count = sum(len(group) for group in groups)
    if count == 1:
        return [("beams", 0), ("exchange", 0), ("own", 0), ("compress", 0), ("send", 0), ("doppler", 0)]
    return [
        ("beams", 0),
        ("exchange", 0),
        ("beams<beams", 0),
        ("beams", 1),
        ("exchange", 1),
        ("beams<compress", (1, 0)),
        ("own", 0),
        ("beams<beams", 1),
        ("beams", 2),
        ("beams<compress", (2, 0)),
        ("compress", 0),
        ("compress<exchange", (0, 2)),
        ("arrived<exchange", (1, 2)),
        ("exchange", 2),
        ("compress", 1),
        ("compress<beams", 1),
        ("send", 0),
        ("beams", 3),
        ("exchange", 3),
        ("beams<compress", (3, 2)),
        ("compress", 2),
        ("compress<own", 3),
        ("own", 3),
        ("compress", 3),
        ("send", 1),
        ("doppler", 0),
        ("doppler", 1),
    ]


def on_device(echoes, steer, code, beam_order, dwell, code_len):
    tiles, owners = lax.axis_size("tile"), lax.axis_size("beam")
    columns = echoes.shape[2]
    beam_total = steer.shape[1]
    pulses = columns // G
    total = pulses * owners
    tile_beams = beam_total // tiles
    own = tile_beams // owners

    values = echoes.astype(jnp.float32)
    power = sum_over(jnp.sum(values * values, axis=(0, 2))[None, :], "beam")

    order, lens, limits = lookup(beam_order, code_len, dwell, tile_beams)
    at = (lax.axis_index("beam") * pulses)[None]
    table = jnp.asarray(phase_table(total).astype(jnp.bfloat16))

    groups = groups_of(G)
    chunks = [chunk for group in groups for chunk in group]
    owner_of = [index for index, group in enumerate(groups) for _ in group]
    firsts = [owner_of.index(index) for index in range(len(groups))]
    own_parts, others, ready, ahead, got, out = {}, {}, {}, {}, {}, None
    for kind, number in order_of(groups):
        if kind == "beams":
            gate, gates = chunks[number]
            with jax.named_scope("beams"):
                picks = tuple(range(1 if number in LATER and tiles > 1 else 0, tiles))
                parts = form_beams(
                    echoes, power, order, steer, G, gate, gates, total * G, tiles, number in STREAMED, picks,
                    9 if number < len(groups[0]) + 1 else 0,
                )
            if len(picks) < tiles:
                parts = [parts[-1], *parts[:-1]]
            own_parts[number], *others[number] = parts
        elif kind == "own":
            if tiles > 1 and number in LATER:
                with jax.named_scope("beams"):
                    own_parts[number] = pick_own(own_parts[number], order, tiles)
        elif kind == "exchange":
            with jax.named_scope("tile_sum"):
                others[number] = [
                    lax.ppermute(part, "tile", [(i, (i + away) % tiles) for i in range(tiles)])
                    for away, part in enumerate(others[number], 1)
                ]
        elif kind == "arrived<exchange":
            others[number[0]][0], others[number[1]][0] = lax.optimization_barrier(
                (others[number[0]][0], others[number[1]][0])
            )
        elif kind == "compress":
            index = owner_of[number]
            place = number - firsts[index]
            with jax.named_scope("compress"):
                ready[index], ahead[number] = compress(
                    [own_parts[number]] + others[number],
                    ahead.get(number - 1), code, at, lens, limits, pulses, owners, number < len(chunks) - 1,
                    ready.get(index), len(groups[index]) - 1 - place, len(groups[index]), 100 if index else 3,
                )
            if ahead[number] is not None:
                with jax.named_scope("edge"):
                    ahead[number] = edge_sums(ahead[number], code, lens, pulses)
        elif kind == "send":
            with jax.named_scope("to_owners"):
                got[number] = lax.all_to_all(ready[number], "beam", split_axis=0, concat_axis=0)
        elif kind == "doppler":
            with jax.named_scope("doppler"):
                out = doppler(got[number], table, out, groups[number][-1][0], pulses)
        elif kind == "beams<beams":
            power, own_parts[number] = lax.optimization_barrier((power, own_parts[number]))
        elif kind == "beams<compress":
            own_parts[number[1]], own_parts[number[0]] = lax.optimization_barrier(
                (own_parts[number[1]], own_parts[number[0]])
            )
        elif kind == "arrived<beams":
            power, others[number][0] = lax.optimization_barrier((power, others[number][0]))
        elif kind == "arrived<doppler":
            table, others[number][0] = lax.optimization_barrier((table, others[number][0]))
        elif kind == "compress<own":
            own_parts[number], ahead = lax.optimization_barrier((own_parts[number], ahead))
        elif kind == "compress<exchange":
            others[number[1]][0], ahead[number[0]] = lax.optimization_barrier(
                (others[number[1]][0], ahead[number[0]])
            )
        elif kind == "compress<beams":
            index = owner_of[number]
            power, ready[index] = lax.optimization_barrier((power, ready[index]))
        elif kind == "compress<doppler":
            table, ahead[number] = lax.optimization_barrier((table, ahead[number]))
        elif kind == "doppler<compress":
            ahead[number], out = lax.optimization_barrier((ahead[number], out))
        elif kind == "last<doppler":
            out, ready[number] = lax.optimization_barrier((out, ready[number]))
    return out


def solution(mesh):
    placed = (P(None, "tile", "beam"), P(None, None, "tile"), P(), P(), P(), P())
    return jax.shard_map(
        on_device,
        mesh=mesh,
        in_specs=placed,
        out_specs=P(("tile", "beam"), None, None, None),
        check_vma=False,
    )
```

```python
import functools
import math

import jax
import jax.numpy as jnp
import numpy as np
from jax import lax
from jax.experimental import pallas as pl
from jax.experimental.pallas import tpu as pltpu
from jax.sharding import PartitionSpec as P

G = 32
EPS = 1e-05
CHUNK = 8
TOGETHER = (2, 2)
STREAMED = (0, 1, 3)
LATER = (0, 3)
NT = (((1,), (1,)), ((), ()))
TN = (((0,), (0,)), ((), ()))
MIB = 1024 * 1024


def params(mib):
    return pltpu.CompilerParams(vmem_limit_bytes=mib * MIB)


def busy(micros):
    return pl.CostEstimate(flops=int(micros * 1.15e9), bytes_accessed=1, transcendentals=0)


def block_of(size, most):
    return max(n for n in range(1, min(size, most) + 1) if size % n == 0)


def groups_of(gates):
    if CHUNK * sum(TOGETHER) != gates:
        return [[(0, gates)]]
    found, end = [], gates
    for count in TOGETHER:
        found.append([(end - CHUNK * (i + 1), CHUNK) for i in range(count)])
        end -= CHUNK * count
    return found


def in_hbm(*values):
    return [pltpu.with_memory_space_constraint(x, pltpu.HBM) for x in values]


def lookup_kernel(order_ref, lens_ref, limits_ref, near_ref, len_ref, limit_ref):
    tiles, mine = lax.axis_size("tile"), lax.axis_index("tile")
    beam_total, slots = order_ref.shape[1], len_ref.shape[1]
    for away in range(tiles):
        start = pl.multiple_of(lax.rem(mine + away, tiles) * slots, slots)
        near_ref[:, away * slots : (away + 1) * slots] = order_ref[:, pl.ds(start, slots)]
    wide = block_of(beam_total, 512)
    found = jnp.zeros((8, slots), jnp.float32)
    for first in range(0, beam_total, wide):
        at = slice(first, first + wide)
        lens, limits = lens_ref[:, at], limits_ref[:, at]
        row = lax.broadcasted_iota(jnp.int32, (8, wide), 0)
        values = jnp.where(row == 0, lens, jnp.where(row == 1, limits >> 5, limits & 31))
        beam = first + lax.broadcasted_iota(jnp.int32, (wide, slots), 0)
        pick = jnp.where(beam == near_ref[:, :slots], 1.0, 0.0).astype(jnp.bfloat16)
        found += jnp.dot(
            values.astype(jnp.float32).astype(jnp.bfloat16), pick, preferred_element_type=jnp.float32
        )
    found = found.astype(jnp.int32)
    len_ref[...] = found[0:1]
    limit_ref[...] = found[1:2] * 32 + found[2:3]


def lookup(order, code_len, dwell, slots):
    whole = pl.BlockSpec(memory_space=pltpu.VMEM)
    return pl.pallas_call(
        lookup_kernel,
        in_specs=[whole] * 3,
        out_specs=[whole] * 3,
        out_shape=[jax.ShapeDtypeStruct((1, size), jnp.int32) for size in (order.shape[0], slots, slots)],
        compiler_params=params(8),
        cost_estimate=busy(20),
        name="lookup",
    )(order[None, :], code_len[None, :], dwell[None, :])


def add_kernel(*refs):
    total = refs[0][...]
    for ref in refs[1:-1]:
        total = total + ref[...]
    refs[-1][...] = total


def add(*values):
    whole = pl.BlockSpec(memory_space=pltpu.VMEM)
    return pl.pallas_call(
        add_kernel,
        in_specs=[whole] * len(values),
        out_specs=whole,
        out_shape=jax.ShapeDtypeStruct(values[0].shape, values[0].dtype),
        compiler_params=params(1),
        cost_estimate=busy(1),
        name="add",
    )(*values)


def beam_kernel(samples, gates, gate, count, streamed, tiles, picks, echoes_ref, power_ref, order_ref, steer_ref, *rest):
    if streamed:
        steer_hbm, steer_ref, sem = steer_ref, rest[-2], rest[-1]
        rest = rest[:-2]
    out_refs, (scaled_ref, row_ref, picked_ref) = rest[:-3], rest[-3:]
    if len(picks) < tiles:
        *out_refs, beams_ref = out_refs
    _, chans, columns = echoes_ref.shape
    beam_total, wide = steer_ref.shape[1], row_ref.shape[0]
    steps = beam_total // wide

    def copy(part, step):
        at = pl.ds(step * wide, wide)
        return pltpu.make_async_copy(steer_hbm.at[part, at], steer_ref.at[part, at], sem.at[part, step])

    if streamed:
        for part in range(2):
            copy(part, 0).start()
    pulses = columns // gates
    rows = count * pulses
    row = lax.broadcasted_iota(jnp.int32, (rows, columns), 0)
    col = lax.broadcasted_iota(jnp.int32, (rows, columns), 1)
    source = (row % pulses) * gates + row // pulses + gate
    moved = jnp.where(source == col, 1.0, 0.0).astype(jnp.bfloat16)
    row_ref[...] = lax.broadcasted_iota(jnp.int32, row_ref.shape, 0)
    gain = lax.rsqrt(power_ref[...] / samples + EPS)
    real = lax.dot_general(moved, echoes_ref[0], NT, preferred_element_type=jnp.float32) * gain
    imag = lax.dot_general(moved, echoes_ref[1], NT, preferred_element_type=jnp.float32) * gain
    scaled_ref[:rows, :chans] = real.astype(jnp.bfloat16)
    scaled_ref[:rows, chans:] = (-imag).astype(jnp.bfloat16)
    scaled_ref[rows:, :chans] = imag.astype(jnp.bfloat16)
    scaled_ref[rows:, chans:] = real.astype(jnp.bfloat16)

    if streamed and steps > 1:
        for part in range(2):
            copy(part, 1).start()
    slots, tile_beams = row_ref.shape[1], beam_total // tiles
    starts = [start for tile in picks for start in range(tile * tile_beams, (tile + 1) * tile_beams, slots)]
    for step in range(steps):
        at = slice(step * wide, (step + 1) * wide)
        if streamed:
            for part in range(2):
                copy(part, step).wait()
                if step + 2 < steps:
                    copy(part, step + 2).start()
        beams = lax.dot_general(scaled_ref[:, :chans], steer_ref[0, at], NT, preferred_element_type=jnp.float32)
        beams += lax.dot_general(scaled_ref[:, chans:], steer_ref[1, at], NT, preferred_element_type=jnp.float32)
        beams = beams.astype(jnp.bfloat16)
        if len(picks) < tiles:
            beams_ref[:, at] = beams
        for start in starts:
            wanted = order_ref[:, start : start + slots] - step * wide
            pick = jnp.where(row_ref[...] == wanted, 1.0, 0.0).astype(jnp.bfloat16)
            picked = jnp.dot(beams, pick, preferred_element_type=jnp.float32)
            if step > 0:
                picked += picked_ref[:, start : start + slots]
            picked_ref[:, start : start + slots] = picked

    for tile, out_ref in zip(picks, out_refs):
        out_ref[...] = picked_ref[:, tile * tile_beams : (tile + 1) * tile_beams].astype(jnp.bfloat16)


def own_kernel(beams_ref, order_ref, out_ref, row_ref):
    beam_total, slots = beams_ref.shape[1], out_ref.shape[1]
    wide, some = row_ref.shape
    row_ref[...] = lax.broadcasted_iota(jnp.int32, row_ref.shape, 0)
    for start in range(0, slots, some):
        picked = None
        for first in range(0, beam_total, wide):
            wanted = order_ref[:, start : start + some] - first
            pick = jnp.where(row_ref[...] == wanted, 1.0, 0.0).astype(jnp.bfloat16)
            term = jnp.dot(beams_ref[:, first : first + wide], pick, preferred_element_type=jnp.float32)
            picked = term if picked is None else picked + term
        out_ref[:, start : start + some] = picked.astype(jnp.bfloat16)


def pick_own(beams, order, tiles):
    rows, beam_total = beams.shape
    slots = beam_total // tiles
    whole = pl.BlockSpec(memory_space=pltpu.VMEM)
    return pl.pallas_call(
        own_kernel,
        in_specs=[whole] * 2,
        out_specs=whole,
        out_shape=pltpu.VMEM((rows, slots), jnp.bfloat16),
        scratch_shapes=[pltpu.VMEM((block_of(beam_total, 512), block_of(slots, 512)), jnp.int32)],
        compiler_params=params(16),
        cost_estimate=busy(2),
        name="own",
    )(pltpu.with_memory_space_constraint(beams, pltpu.VMEM), order)


def form_beams(echoes, power, order, steer, gates, gate, count, samples, tiles, streamed, picks, micros):
    _, chans, columns = echoes.shape
    beam_total = steer.shape[1]
    tile_beams = beam_total // tiles
    rows = columns // gates * count
    wide = block_of(beam_total, 512)
    echoes = pltpu.with_memory_space_constraint(echoes, pltpu.VMEM)
    steer = pltpu.with_memory_space_constraint(steer, pltpu.HBM if streamed else pltpu.VMEM)
    whole = pl.BlockSpec(memory_space=pltpu.VMEM)
    spaces = [pltpu.HBM if tile else pltpu.VMEM for tile in picks]
    out_shape = [space((2 * rows, tile_beams), jnp.bfloat16) for space in spaces]
    if len(picks) < tiles:
        out_shape.append(pltpu.VMEM((2 * rows, beam_total), jnp.bfloat16))
    return pl.pallas_call(
        functools.partial(beam_kernel, samples, gates, gate, count, streamed, tiles, picks),
        in_specs=[whole] * 3 + [pl.BlockSpec(memory_space=pl.ANY) if streamed else whole],
        out_specs=[whole] * len(out_shape),
        out_shape=out_shape,
        scratch_shapes=[
            pltpu.VMEM((2 * rows, 2 * chans), jnp.bfloat16),
            pltpu.VMEM((wide, block_of(tile_beams, 512)), jnp.int32),
            pltpu.VMEM((2 * rows, beam_total), jnp.float32),
        ]
        + ([pltpu.VMEM(steer.shape, steer.dtype), pltpu.SemaphoreType.DMA((2, beam_total // wide))] if streamed else []),
        compiler_params=params(24),
        cost_estimate=busy(micros),
        name="beams",
    )(echoes, power, order, steer)


def factors_of(code_ref, lens, taps):
    code = code_ref[...].astype(jnp.float32)
    return [
        tuple(jnp.where(tap < lens, code[part : part + 1, tap : tap + 1], 0.0) for part in range(2))
        for tap in range(taps)
    ]


def add_tap(real, imag, factor, shift_re, shift_im):
    code_re, code_im = factor
    term_re = code_re * shift_re + code_im * shift_im
    term_im = code_re * shift_im - code_im * shift_re
    return (term_re, term_im) if real is None else (real + term_re, imag + term_im)


def edge_kernel(pulses, taps, lanes, code_ref, lens_ref, ahead_ref, sums_ref):
    for first in range(0, lens_ref.shape[1], lanes):
        at = slice(first, first + lanes)
        factors = factors_of(code_ref, lens_ref[:, at], taps)
        after = [
            [ahead_ref[part, i * pulses : (i + 1) * pulses, at].astype(jnp.float32) for part in range(2)]
            for i in range(taps - 1)
        ]
        for gate in range(taps - 1):
            real = imag = None
            for i in range(gate + 1):
                real, imag = add_tap(real, imag, factors[taps - 1 - gate + i], *after[i])
            sums_ref[0, gate * pulses : (gate + 1) * pulses, at] = real
            sums_ref[1, gate * pulses : (gate + 1) * pulses, at] = imag


def edge_sums(ahead, code, lens, pulses):
    whole = pl.BlockSpec(memory_space=pltpu.VMEM)
    return pl.pallas_call(
        functools.partial(edge_kernel, pulses, code.shape[1], block_of(lens.shape[1], 256)),
        in_specs=[whole] * 3,
        out_specs=whole,
        out_shape=pltpu.VMEM(ahead.shape, jnp.float32),
        compiler_params=params(16),
        cost_estimate=busy(1),
        name="edge",
    )(code, lens, pltpu.with_memory_space_constraint(ahead, pltpu.VMEM))


def compress_kernel(pulses, taps, parts_in, halo, shared, keep_ahead, place, code_ref, at_ref, lens_ref, limits_ref, *rest):
    part_refs, rest = rest[:parts_in], rest[parts_in:]
    if halo:
        sums_ref, rest = rest[0], rest[1:]
    out_hbm, rest = rest[shared], rest[shared + 1 :]
    away = keep_ahead and place == 0
    if away:
        beams_hbm, beams_ref, beams_sem, rest = rest[0], rest[-2], rest[-1], rest[1:-2]
    elif keep_ahead:
        beams_ref, rest = rest[0], rest[1:]
    wide_ref, laid_ref, sem = rest
    rows, tile_beams = part_refs[0].shape[0] // 2, part_refs[0].shape[1]
    edge = (taps - 1) * pulses
    lanes = wide_ref.shape[2]
    own = laid_ref.shape[2] // 2
    some = lanes // own

    def copy(block):
        at = pl.ds(block * some, some)
        return pltpu.make_async_copy(
            laid_ref.at[at], out_hbm.at[at, pl.ds(place * rows, rows)], sem.at[block]
        )

    def beams_copy(block):
        at = pl.ds(block * lanes, lanes)
        return pltpu.make_async_copy(beams_ref.at[:, :, at], beams_hbm.at[:, :, at], beams_sem.at[block])

    for block in range(tile_beams // lanes):
        at = slice(block * lanes, (block + 1) * lanes)
        for part in range(2):
            total = part_refs[0][part * rows : (part + 1) * rows, at].astype(jnp.float32)
            for ref in part_refs[1:]:
                total += ref[part * rows : (part + 1) * rows, at].astype(jnp.float32)
            rounded = total.astype(jnp.bfloat16)
            if keep_ahead:
                beams_ref[part, :, at] = rounded[:edge]
            wide_ref[part] = rounded.astype(jnp.float32)
        if away:
            beams_copy(block).start()
        lens, limits = lens_ref[:, at], limits_ref[:, at]
        pulse = at_ref[0] + lax.broadcasted_iota(jnp.int32, (pulses, lanes), 0)
        keep = pulse < limits
        factors = factors_of(code_ref, lens, taps)
        gates = rows // pulses
        for gate in range(gates):
            real = imag = None
            before = gate - (gates - taps + 1)
            if halo and before >= 0:
                real = sums_ref[0, before * pulses : (before + 1) * pulses, at]
                imag = sums_ref[1, before * pulses : (before + 1) * pulses, at]
            for tap in range(min(taps, gates - gate)):
                start = (gate + tap) * pulses
                real, imag = add_tap(
                    real, imag, factors[tap], wide_ref[0, start : start + pulses], wide_ref[1, start : start + pulses]
                )
            real = jnp.where(keep, real, 0.0)
            imag = jnp.where(keep, imag, 0.0)
            for owner in range(some):
                line = slice(owner * own, (owner + 1) * own)
                joined = jnp.concatenate([real[:, line], imag[:, line]], axis=1).astype(jnp.bfloat16)
                laid_ref[block * some + owner, gate * pulses : (gate + 1) * pulses] = joined
        copy(block).start()
    for block in range(tile_beams // lanes):
        copy(block).wait()
        if away:
            beams_copy(block).wait()


def compress(parts, ahead, code, at, lens, limits, pulses, owners, keep_ahead, ready, place, places, micros):
    taps = code.shape[1]
    rows, tile_beams = parts[0].shape[0] // 2, parts[0].shape[1]
    own = tile_beams // owners
    lanes = block_of(tile_beams, 256)
    edge = (taps - 1) * pulses
    whole, apart = pl.BlockSpec(memory_space=pltpu.VMEM), pl.BlockSpec(memory_space=pl.ANY)
    scalars = pl.BlockSpec(memory_space=pltpu.SMEM)
    out_shape = [pltpu.HBM((owners, places * rows, 2 * own), jnp.bfloat16)]
    if keep_ahead:
        out_shape.append((pltpu.VMEM if place else pltpu.HBM)((2, edge, tile_beams), jnp.bfloat16))
    near = [pltpu.with_memory_space_constraint(x, pltpu.VMEM) for x in parts + ([] if ahead is None else [ahead])]
    shared = [] if ready is None else in_hbm(ready)
    done = pl.pallas_call(
        functools.partial(
            compress_kernel, pulses, taps, len(parts), ahead is not None, len(shared), keep_ahead, place
        ),
        in_specs=[whole, scalars, whole, whole] + [whole] * len(near) + [apart] * len(shared),
        out_specs=[apart] + [whole if place else apart] * keep_ahead,
        out_shape=out_shape,
        scratch_shapes=[
            pltpu.VMEM((2, rows, lanes), jnp.float32),
            pltpu.VMEM((owners, rows, 2 * own), jnp.bfloat16),
            pltpu.SemaphoreType.DMA((tile_beams // lanes,)),
        ]
        + (
            [pltpu.VMEM((2, edge, tile_beams), jnp.bfloat16), pltpu.SemaphoreType.DMA((tile_beams // lanes,))]
            if keep_ahead and place == 0
            else []
        ),
        input_output_aliases={4 + len(near): 0} if shared else {},
        compiler_params=params(16),
        cost_estimate=busy(micros),
        name="compress",
    )(code, at, lens, limits, *near, *shared)
    return done if keep_ahead else (done[0], None)


def doppler_kernel(pulses, first, some, got_ref, table_ref, *rest):
    out_hbm, lines_ref, block_ref, sem = rest[-4:]
    owners, rows, lanes = got_ref.shape
    own, bins = lanes // 2, table_ref.shape[1] // 2
    gates = rows // pulses
    batch = block_of(some, max(1, 256 // lanes))

    def copy(block):
        at = pl.ds(first + block * some, some)
        return pltpu.make_async_copy(block_ref.at[block], out_hbm.at[:, :, at], sem.at[block])

    for block in range(gates // some):
        for start in range(0, some, batch):
            values = jnp.concatenate(
                [
                    got_ref[:, gate * pulses : (gate + 1) * pulses].reshape(owners * pulses, lanes)
                    for gate in range(block * some + start, block * some + start + batch)
                ],
                axis=1,
            )
            both = lax.dot_general(values, table_ref[...], TN, preferred_element_type=jnp.float32)
            for index in range(batch):
                upper = both[index * lanes : index * lanes + own]
                lower = both[index * lanes + own : (index + 1) * lanes]
                real = upper[:, :bins] - lower[:, bins:]
                imag = lower[:, :bins] + upper[:, bins:]
                for part, line in enumerate((real, imag)):
                    for at in range(lines_ref.shape[0]):
                        to = pl.ds(part * some + start + index, own, stride=2 * some)
                        lines_ref[at, to, :] = line[:, at * 128 : (at + 1) * 128]
        for at in range(lines_ref.shape[0]):
            block_ref[block, :, :, :, at * 128 : (at + 1) * 128] = lines_ref[at].reshape(own, 2, some, 128)
        copy(block).start()
    for block in range(gates // some):
        copy(block).wait()


def doppler(got, table, out, first, pulses):
    owners, rows, lanes = got.shape
    own, bins, gates = lanes // 2, table.shape[1] // 2, rows // pulses
    some = CHUNK if gates % CHUNK == 0 else gates
    whole, apart = pl.BlockSpec(memory_space=pltpu.VMEM), pl.BlockSpec(memory_space=pl.ANY)
    before = [] if out is None else [out]
    return pl.pallas_call(
        functools.partial(doppler_kernel, pulses, first, some),
        in_specs=[whole, whole] + [apart] * len(before),
        out_specs=apart,
        out_shape=jax.ShapeDtypeStruct((own, 2, G, bins), jnp.float32),
        scratch_shapes=[
            pltpu.VMEM((bins // 128, own * 2 * some, 128), jnp.float32),
            pltpu.VMEM((gates // some, own, 2, some, bins), jnp.float32),
            pltpu.SemaphoreType.DMA((gates // some,)),
        ],
        input_output_aliases={2: 0} if before else {},
        compiler_params=params(24),
        cost_estimate=busy(3),
        name="doppler",
    )(pltpu.with_memory_space_constraint(got, pltpu.VMEM), table, *before)


def phase_table(total):
    angle = np.outer(np.arange(total), np.arange(total)) % total * (2.0 * math.pi / total)
    return np.concatenate([np.cos(angle), -np.sin(angle)], axis=1) / math.sqrt(total)


def sum_over(values, axis):
    size = lax.axis_size(axis)
    if size & (size - 1):
        return lax.psum(values, axis)
    step = 1
    while step < size:
        steps = [step * i for i in (1, 2, 3) if step * i < size] if step * 2 < size else [step]
        values = add(
            values, *(lax.ppermute(values, axis, [(i, i ^ away) for i in range(size)]) for away in steps)
        )
        step *= len(steps) + 1
    return values


def order_of(groups):
    count = sum(len(group) for group in groups)
    if count == 1:
        return [("beams", 0), ("exchange", 0), ("own", 0), ("compress", 0), ("send", 0), ("doppler", 0)]
    return [
        ("beams", 0),
        ("exchange", 0),
        ("beams<beams", 0),
        ("beams", 1),
        ("exchange", 1),
        ("beams<compress", (1, 0)),
        ("own", 0),
        ("beams<beams", 1),
        ("beams", 2),
        ("beams<compress", (2, 0)),
        ("compress", 0),
        ("compress<exchange", (0, 2)),
        ("arrived<exchange", (1, 2)),
        ("exchange", 2),
        ("compress", 1),
        ("compress<beams", 1),
        ("send", 0),
        ("beams", 3),
        ("exchange", 3),
        ("beams<compress", (3, 2)),
        ("compress", 2),
        ("compress<own", 3),
        ("own", 3),
        ("compress", 3),
        ("send", 1),
        ("doppler", 0),
        ("doppler", 1),
    ]


def on_device(echoes, steer, code, beam_order, dwell, code_len):
    tiles, owners = lax.axis_size("tile"), lax.axis_size("beam")
    columns = echoes.shape[2]
    beam_total = steer.shape[1]
    pulses = columns // G
    total = pulses * owners
    tile_beams = beam_total // tiles
    own = tile_beams // owners

    values = echoes.astype(jnp.float32)
    power = sum_over(jnp.sum(values * values, axis=(0, 2))[None, :], "beam")

    order, lens, limits = lookup(beam_order, code_len, dwell, tile_beams)
    at = (lax.axis_index("beam") * pulses)[None]
    table = jnp.asarray(phase_table(total).astype(jnp.bfloat16))

    groups = groups_of(G)
    chunks = [chunk for group in groups for chunk in group]
    owner_of = [index for index, group in enumerate(groups) for _ in group]
    firsts = [owner_of.index(index) for index in range(len(groups))]
    own_parts, others, ready, ahead, got, out = {}, {}, {}, {}, {}, None
    for kind, number in order_of(groups):
        if kind == "beams":
            gate, gates = chunks[number]
            with jax.named_scope("beams"):
                picks = tuple(range(1 if number in LATER and tiles > 1 else 0, tiles))
                parts = form_beams(
                    echoes, power, order, steer, G, gate, gates, total * G, tiles, number in STREAMED, picks,
                    9 if number < len(groups[0]) + 1 else 0,
                )
            if len(picks) < tiles:
                parts = [parts[-1], *parts[:-1]]
            own_parts[number], *others[number] = parts
        elif kind == "own":
            if tiles > 1 and number in LATER:
                with jax.named_scope("beams"):
                    own_parts[number] = pick_own(own_parts[number], order, tiles)
        elif kind == "exchange":
            with jax.named_scope("tile_sum"):
                others[number] = [
                    lax.ppermute(part, "tile", [(i, (i + away) % tiles) for i in range(tiles)])
                    for away, part in enumerate(others[number], 1)
                ]
        elif kind == "arrived<exchange":
            others[number[0]][0], others[number[1]][0] = lax.optimization_barrier(
                (others[number[0]][0], others[number[1]][0])
            )
        elif kind == "compress":
            index = owner_of[number]
            place = number - firsts[index]
            with jax.named_scope("compress"):
                ready[index], ahead[number] = compress(
                    [own_parts[number]] + others[number],
                    ahead.get(number - 1), code, at, lens, limits, pulses, owners, number < len(chunks) - 1,
                    ready.get(index), len(groups[index]) - 1 - place, len(groups[index]), 100 if index else 3,
                )
            if ahead[number] is not None:
                with jax.named_scope("edge"):
                    ahead[number] = edge_sums(ahead[number], code, lens, pulses)
        elif kind == "send":
            with jax.named_scope("to_owners"):
                got[number] = lax.all_to_all(ready[number], "beam", split_axis=0, concat_axis=0)
        elif kind == "doppler":
            with jax.named_scope("doppler"):
                out = doppler(got[number], table, out, groups[number][-1][0], pulses)
        elif kind == "beams<beams":
            power, own_parts[number] = lax.optimization_barrier((power, own_parts[number]))
        elif kind == "beams<compress":
            own_parts[number[1]], own_parts[number[0]] = lax.optimization_barrier(
                (own_parts[number[1]], own_parts[number[0]])
            )
        elif kind == "arrived<beams":
            power, others[number][0] = lax.optimization_barrier((power, others[number][0]))
        elif kind == "arrived<doppler":
            table, others[number][0] = lax.optimization_barrier((table, others[number][0]))
        elif kind == "compress<own":
            own_parts[number], ahead = lax.optimization_barrier((own_parts[number], ahead))
        elif kind == "compress<exchange":
            others[number[1]][0], ahead[number[0]] = lax.optimization_barrier(
                (others[number[1]][0], ahead[number[0]])
            )
        elif kind == "compress<beams":
            index = owner_of[number]
            power, ready[index] = lax.optimization_barrier((power, ready[index]))
        elif kind == "compress<doppler":
            table, ahead[number] = lax.optimization_barrier((table, ahead[number]))
        elif kind == "doppler<compress":
            ahead[number], out = lax.optimization_barrier((ahead[number], out))
        elif kind == "last<doppler":
            out, ready[number] = lax.optimization_barrier((out, ready[number]))
    return out


def solution(mesh):
    placed = (P(None, "tile", "beam"), P(None, None, "tile"), P(), P(), P(), P())
    return jax.shard_map(
        on_device,
        mesh=mesh,
        in_specs=placed,
        out_specs=P(("tile", "beam"), None, None, None),
        check_vma=False,
    )
```
